256 devices in a mesh: pipe: 2 (over core), tensor: 4 (over x), dp: 32 (over z, y).
Axes of the slice: x: 4, y: 4, z: 8, core: 2. Of those that a mesh axis runs over, the one named last changes fastest.
Arguments:
- section_input: bfloat16 [2, 4096, 4096], P('pipe', 'dp'), may hold values from -8 to 8
- norm_gain: float32 [2, 4096], P('pipe'), may hold values from 0.25 to 1.75
- cotangent: bfloat16 [4096, 4096], P('dp'), may hold values from -6 to 6
- qkv_base: bfloat16 [2, 5120, 4096], P('pipe', 'tensor', 'dp'), may hold values from -1 to 1
- qkv_sign: bfloat16 [2, 5120, 4096], P('pipe', 'tensor', 'dp'), may hold values from -1 to 1, as said below
- qkv_scale: float32 [2, 5120], P('pipe', 'tensor'), may hold values from 0.002 to 0.02
- out_base: bfloat16 [2, 4096, 4096], P('pipe', None, 'tensor'), may hold values from -0.09375 to 0.09375
Outputs:
- qkv_scale_grad: float32 [2, 5120], P('pipe', 'tensor')
The draws below stay inside these ranges and needn't reach their ends.
Inputs may be any that keep to these rules, and one draw needn't show every extreme that they name: `qkv_sign`: every entry is -1 or +1.
All inputs are finite; a program needn't handle non-finite values.
Results may differ from the reference program's by a relative error of at most 0.02.
Values may be sent and summed in bfloat16 or wider, within the bound.
No kernel may reach another device: no remote copies, remote signals or barrier semaphores. Data moves between devices by JAX's collectives and lax.ppermute only.
A program may use at most 128 MiB of HBM per device.

```python
import math
import jax
import jax.numpy as jnp
from jax import lax

D = 4096
HD = 128
QH = 8
LEN = 128
LAYERS = 2
QKV_DEV = 1280
QKV = 5120
HT = 4096
TOKENS = 4096
N_PIPE = 2
N_TENSOR = 4
N_DP = 32


def draw_qkv_sign(key, part):
    key = jax.random.fold_in(key, 11)
    coin_flips = jax.random.randint(key, (LAYERS, QKV, D), 0, 2)
    return (2 * coin_flips - 1).astype(jnp.float32).astype(jnp.bfloat16)


def draw_qkv_base(key, part):
    key = jax.random.fold_in(key, 37)
    spread = D ** (-0.5)
    values = jnp.clip(jax.random.normal(key, (LAYERS, QKV, D), jnp.float32), -6.0, 6.0) * spread
    return values.astype(jnp.bfloat16)


def draw_section_input(key, part):
    key = jax.random.fold_in(key, 41)
    noise_key = jax.random.fold_in(key, 0)
    values = jnp.clip(jax.random.normal(noise_key, (LAYERS, TOKENS, D), jnp.float32), -6.0, 6.0)
    return values.astype(jnp.bfloat16)


def shard_levels(key, dims, cuts, low, top_value):
    gain, own = 1.0, jax.random.fold_in(key, 6)
    for dim, parts in cuts:
        heights = jnp.exp(jax.random.uniform(jax.random.fold_in(own, dim), (parts,), jnp.float32, low / len(cuts), top_value / len(cuts)))
        gain = gain * jnp.repeat(heights, dims[dim] // parts).reshape([-1 if axis == dim else 1 for axis in range(len(dims))])
    return gain


def normal_values(key, shape, width, most, cuts=(), held_as=jnp.bfloat16):
    level = shard_levels(key, shape, cuts, -0.22, 0.18) if cuts else 1.0
    result = jax.random.normal(key, shape, jnp.float32) * width * level
    return jnp.minimum(jnp.maximum(result, -most), most).astype(held_as)


def setup_inputs(seed: int = 0) -> dict:
    streams_of = jax.random.split(jax.random.key(seed), 8)
    return {
        "section_input": draw_section_input(jax.random.fold_in(streams_of[7], 71), 0),
        "norm_gain": jnp.clip(1.0 + 0.15 * jax.random.normal(streams_of[1], (LAYERS, D), jnp.float32), 0.25, 1.75),
        "cotangent": normal_values(streams_of[2], (TOKENS, D), 1.0, 6.0, ((0, 32),)),
        "qkv_base": draw_qkv_base(jax.random.fold_in(streams_of[7], 71), 0),
        "qkv_sign": draw_qkv_sign(jax.random.fold_in(streams_of[7], 71), 0),
        "qkv_scale": jnp.clip(jnp.exp(math.log(0.02) - 2.30258502 * jax.random.uniform(streams_of[5], (LAYERS, QKV), jnp.float32) ** shard_levels(streams_of[5], (LAYERS, QKV), ((0, 2), (1, 4)), -0.2, 0.2)), 0.002, 0.02),
        "out_base": normal_values(streams_of[6], (LAYERS, D, HT), HT ** -0.5, 0.09375, ((0, 2), (2, 4))),
    }


def norm_parts(inputs, gain_row):
    values = inputs.astype(jnp.float32)
    factor = lax.rsqrt(lax.optimization_barrier(jnp.mean(values * values, axis=-1, keepdims=True)) + 1e-05)
    normed = values * factor
    return ((normed * gain_row).astype(jnp.bfloat16), normed, factor)

def norm_back(grad_hidden, normed, factor, gain_row):
    grad_normed = grad_hidden * gain_row
    return factor * (grad_normed - normed * lax.optimization_barrier(jnp.mean(grad_normed * normed, axis=-1, keepdims=True)))

def split_heads(packed, head_count, head_width):
    queries = packed[..., :head_count * head_width]
    queries = jnp.moveaxis(queries.reshape(packed.shape[:-1] + (head_count, head_width)), -2, -3)
    key_rows = packed[..., head_count * head_width:(head_count + 1) * head_width]
    value_rows = packed[..., (head_count + 1) * head_width:]
    return (queries, key_rows, value_rows)

def merge_heads(heads_in):
    moved = jnp.moveaxis(heads_in, -3, -2)
    return moved.reshape(moved.shape[:-2] + (moved.shape[-2] * moved.shape[-1],))

def attend(queries, key_rows, value_rows):
    head_width = queries.shape[-1]
    seq_length = queries.shape[-2]
    scores = jnp.einsum('...hqd,...kd->...hqk', queries, key_rows) / math.sqrt(head_width)
    row_ids = lax.broadcasted_iota(jnp.int32, (seq_length, seq_length), 0)
    col_ids = lax.broadcasted_iota(jnp.int32, (seq_length, seq_length), 1)
    scores = jnp.where(col_ids <= row_ids, scores, -1000000000.0)
    weights = jax.nn.softmax(scores, axis=-1)
    return jnp.einsum('...hqk,...kd->...hqd', weights, value_rows)

def reference(section_input, norm_gain, cotangent, qkv_base, qkv_sign, qkv_scale, out_base):
    groups = N_TENSOR
    sequences = N_DP
    grad_y = cotangent
    totals_q = []
    for layer in range(N_PIPE - 1, -1, -1):
        gain_row = norm_gain[layer].astype(jnp.float32)
        weight_qkv = (qkv_base[layer].astype(jnp.float32) + qkv_scale[layer][:, None] * qkv_sign[layer].astype(jnp.float32)).astype(jnp.bfloat16)
        weight_out = out_base[layer]
        hidden, normed, factor = norm_parts(section_input[layer], gain_row)
        packed = jnp.dot(hidden, weight_qkv.T, preferred_element_type=jnp.float32).astype(jnp.bfloat16)
        grouped = jnp.moveaxis(packed.reshape(sequences, LEN, groups, QKV_DEV), 2, 1).astype(jnp.float32)
        queries, key_rows, value_rows = split_heads(grouped, QH, HD)
        attended, attend_back = jax.vjp(attend, queries, key_rows, value_rows)
        grad_mixed = jnp.dot(grad_y, weight_out, preferred_element_type=jnp.float32).astype(jnp.bfloat16)
        grad_heads = grad_mixed.astype(jnp.float32).reshape(sequences, LEN, groups, QH, HD)
        grad_heads = jnp.moveaxis(jnp.moveaxis(grad_heads, 2, 1), 3, 2)
        grad_q, grad_k, grad_v = attend_back(grad_heads)
        grad_grouped = jnp.concatenate([merge_heads(grad_q), grad_k, grad_v], axis=-1).astype(jnp.bfloat16)
        grad_packed = jnp.moveaxis(grad_grouped, 1, 2).reshape(TOKENS, QKV)
        weight_grad_q = jnp.dot(grad_packed.T, hidden, preferred_element_type=jnp.float32)
        totals_q.append(lax.optimization_barrier(jnp.sum(weight_grad_q * qkv_sign[layer].astype(jnp.float32), axis=1)) / TOKENS)
        if layer > 0:
            weight_groups = weight_qkv.reshape(groups, QKV_DEV, D).astype(jnp.float32)
            grad_groups = grad_packed.reshape(TOKENS, groups, QKV_DEV).astype(jnp.float32)
            group_terms = jnp.einsum('tgc,gcd->tgd', grad_groups, weight_groups).astype(jnp.bfloat16)
            grad_hidden = lax.optimization_barrier(jnp.sum(group_terms, axis=1, dtype=jnp.float32))
            grad_y = (grad_y.astype(jnp.float32) + norm_back(grad_hidden, normed, factor, gain_row)).astype(jnp.bfloat16)
    return jnp.stack(totals_q[::-1])
```

```python
import functools
import math

import jax
import jax.numpy as jnp
from jax import lax
from jax.experimental import pallas as pl
from jax.experimental.pallas import tpu as pltpu
from jax.sharding import Mesh
from jax.sharding import PartitionSpec as P

HD = 128
QH = 8
NY = 4
NX = 4

F32 = jnp.float32
BF16 = jnp.bfloat16


def dot_nn(a, b):
    return lax.dot_general(a, b, (((1,), (0,)), ((), ())), preferred_element_type=F32)


def dot_nt(a, b):
    return lax.dot_general(a, b, (((1,), (1,)), ((), ())), preferred_element_type=F32)


def dot_tn(a, b):
    return lax.dot_general(a, b, (((0,), (0,)), ((), ())), preferred_element_type=F32)


def attention_back_kernel(packed_ref, grad_ref, out_ref):
    length = packed_ref.shape[0]
    factor = 1.0 / math.sqrt(HD)
    queries = jnp.concatenate([packed_ref[:, h * HD : (h + 1) * HD] for h in range(QH)], axis=0)
    grads = jnp.concatenate([grad_ref[:, h * HD : (h + 1) * HD] for h in range(QH)], axis=0)
    keys = packed_ref[:, QH * HD : (QH + 1) * HD]
    values = packed_ref[:, (QH + 1) * HD :]
    scores = dot_nt(queries, keys) * factor
    rows = lax.broadcasted_iota(jnp.int32, scores.shape, 0) % length
    cols = lax.broadcasted_iota(jnp.int32, scores.shape, 1)
    scores = jnp.where(cols <= rows, scores, -1000000000.0)
    top = jnp.max(scores, axis=-1, keepdims=True)
    raised = jnp.exp(scores - top)
    weights = raised / jnp.sum(raised, axis=-1, keepdims=True)
    grad_weights = dot_nt(grads, values)
    inner = jnp.sum(grad_weights * weights, axis=-1, keepdims=True)
    grad_scores = (weights * (grad_weights - inner) * factor).astype(BF16)
    grad_queries = dot_nn(grad_scores, keys)
    for h in range(QH):
        out_ref[:, h * HD : (h + 1) * HD] = grad_queries[h * length : (h + 1) * length].astype(BF16)
    out_ref[:, QH * HD : (QH + 1) * HD] = dot_tn(grad_scores, queries).astype(BF16)
    out_ref[:, (QH + 1) * HD :] = dot_tn(weights.astype(BF16), grads).astype(BF16)


def attention_back(packed, grad_mixed):
    return pl.pallas_call(
        attention_back_kernel,
        out_shape=jax.ShapeDtypeStruct(packed.shape, BF16),
        in_specs=[pl.BlockSpec(memory_space=pltpu.VMEM)] * 2,
        out_specs=pl.BlockSpec(memory_space=pltpu.VMEM),
        compiler_params=pltpu.CompilerParams(vmem_limit_bytes=32 * 1024 * 1024),
        cost_estimate=pl.CostEstimate(flops=2 * 5 * 1024 * 128 * 128, bytes_accessed=1000000, transcendentals=131072),
    )(packed, grad_mixed)


def send_y(value, steps):
    return lax.ppermute(value, "y", [(i, (i + steps) % NY) for i in range(NY)])


def send_y_upper(value, steps):
    return lax.ppermute(
        value, ("pipe", "y"), [(NY + i, NY + (i + steps) % NY) for i in range(NY)]
    )


def send_x_upper(value, steps):
    return lax.ppermute(
        value, ("pipe", "tensor"), [(NX + i, NX + (i + steps) % NX) for i in range(NX)]
    )


def send_down(value, steps):
    return lax.ppermute(
        value, ("pipe", "tensor"), [(NX + i, (i + steps) % NX) for i in range(NX)]
    )


def turned(blocks, start):
    doubled = jnp.concatenate([blocks, blocks], axis=0)
    return lax.dynamic_slice_in_dim(doubled, start, blocks.shape[0], 0)


def summed_over_y(partial):
    own = partial.shape[0] // NY
    parts = partial.astype(BF16)
    total = partial[:own]
    for k in range(1, NY):
        total = total + send_y(parts[k * own : (k + 1) * own], -k).astype(F32)
    return total


def local(section_input, norm_gain, cotangent, qkv_base, qkv_sign, qkv_scale, out_base):
    inputs = section_input[0]
    gain_row = norm_gain[0][None, :]
    tokens, width = inputs.shape
    nz = lax.axis_size("z")
    piece = width // (nz * NY)
    slab = nz * piece
    chunk = tokens // NX
    pipe_index = lax.axis_index("pipe")
    x_index = lax.axis_index("tensor")
    y_index = lax.axis_index("y")
    weight_out = out_base[0]

    sign = qkv_sign[0]
    weight = (qkv_base[0].astype(F32) + qkv_scale[0][:, None] * sign.astype(F32)).astype(BF16)
    weight_slab = lax.all_gather(weight.T, "z", axis=0, tiled=True)
    sign_slab = lax.all_gather(sign.T, "z", axis=0, tiled=True)

    values = inputs.astype(F32)
    factor = lax.rsqrt(jnp.mean(values * values, axis=-1, keepdims=True) + 1e-05)
    hidden = (values * factor * gain_row).astype(BF16)
    by_y = hidden.reshape(tokens, nz, NY, piece).transpose(2, 0, 1, 3).reshape(NY, tokens, slab)
    by_y = turned(by_y, y_index)
    hidden_slab = jnp.concatenate([by_y[0]] + [send_y(by_y[k], k) for k in range(1, NY)], axis=0)

    packed = summed_over_y(dot_nn(hidden_slab, weight_slab)).astype(BF16)
    projected = summed_over_y(dot_nn(hidden_slab, sign_slab))

    grad_mixed = dot_nn(cotangent, weight_out).astype(BF16)
    grad_upper = attention_back(packed, grad_mixed)

    sent = turned(grad_upper.reshape(NX, chunk, -1), x_index)
    slab_rows = jnp.stack([sent] + [send_y_upper(sent, k) for k in range(1, NY)], axis=1)
    slab_rows = slab_rows.reshape(NX * NY * chunk, -1)
    back = dot_nt(slab_rows, weight_slab)
    back = back.reshape(NX, NY * chunk, slab)
    back_sent = back.astype(BF16)
    total = back[0]
    for j in range(1, NX):
        total = total + send_x_upper(back_sent[j], j).astype(F32)
    total = total.astype(BF16).reshape(NY, chunk, slab)
    whole = jnp.stack([total[0]] + [send_y_upper(total[k], -k) for k in range(1, NY)], axis=0)
    whole = turned(whole, (NY - y_index) % NY)
    grad_hidden = (
        whole.reshape(NY, chunk, nz, piece).transpose(1, 2, 0, 3).reshape(chunk, width).astype(F32)
    )
    rows = lax.dynamic_slice_in_dim(values, x_index * chunk, chunk, 0)
    rows_factor = lax.dynamic_slice_in_dim(factor, x_index * chunk, chunk, 0)
    rows_grad = lax.dynamic_slice_in_dim(cotangent, x_index * chunk, chunk, 0).astype(F32)
    normed = rows * rows_factor
    grad_normed = grad_hidden * gain_row
    backward = rows_grad + rows_factor * (
        grad_normed - normed * jnp.mean(grad_normed * normed, axis=-1, keepdims=True)
    )
    backward = backward.astype(BF16)
    arrived = [send_down(backward, j) for j in (0, 3, 2, 1)]
    arrived = jnp.concatenate(arrived, axis=0)
    grad_mixed_lower = dot_nn(arrived, weight_out).astype(BF16)
    grad_mixed_lower = turned(grad_mixed_lower.reshape(NX, chunk, -1), (NX - x_index) % NX)
    grad_lower = attention_back(packed, grad_mixed_lower.reshape(tokens, -1))

    kept = jnp.where(pipe_index == 1, grad_upper, grad_lower).astype(F32)
    count = tokens * nz * NY
    partial = jnp.sum(kept * projected, axis=0) * (1.0 / count)
    result = lax.psum(lax.psum(partial, "y"), "z")
    return result[None]


def solution(mesh):
    sizes = mesh.devices.shape
    fine = Mesh(mesh.devices.reshape(sizes[0], sizes[1], sizes[2] // NY, NY), ("pipe", "tensor", "z", "y"))
    dp = ("z", "y")
    placed = (
        P("pipe", dp, None),
        P("pipe", None),
        P(dp, None),
        P("pipe", "tensor", dp),
        P("pipe", "tensor", dp),
        P("pipe", "tensor"),
        P("pipe", None, "tensor"),
    )
    return jax.shard_map(
        local, mesh=fine, in_specs=placed, out_specs=P("pipe", "tensor"), check_vma=False
    )
```

```python
import functools
import math

import jax
import jax.numpy as jnp
from jax import lax
from jax.experimental import pallas as pl
from jax.experimental.pallas import tpu as pltpu
from jax.sharding import Mesh
from jax.sharding import PartitionSpec as P

HD = 128
QH = 8
NY = 4
NX = 4
NZ = 8
ORDER = (0, 7, 1, 6, 2, 5, 3, 4)

F32 = jnp.float32
BF16 = jnp.bfloat16
VMEM = pl.BlockSpec(memory_space=pltpu.VMEM)


def dot_nn(a, b):
    return lax.dot_general(a, b, (((1,), (0,)), ((), ())), preferred_element_type=F32)


def dot_nt(a, b):
    return lax.dot_general(a, b, (((1,), (1,)), ((), ())), preferred_element_type=F32)


def dot_tn(a, b):
    return lax.dot_general(a, b, (((0,), (0,)), ((), ())), preferred_element_type=F32)


def call(kernel, outs, args, flops, vmem=40):
    return pl.pallas_call(
        kernel,
        out_shape=outs,
        in_specs=[VMEM] * len(args),
        out_specs=jax.tree.map(lambda _: VMEM, outs),
        compiler_params=pltpu.CompilerParams(vmem_limit_bytes=vmem * 1024 * 1024),
        cost_estimate=pl.CostEstimate(flops=flops, bytes_accessed=100000, transcendentals=0),
    )(*args)


def block_column(z_index, y_index, y_step, z_step):
    block = ((z_index + z_step) % NZ) * NY + (y_index + y_step) % NY
    return pl.multiple_of(block * HD, HD)


def norm_kernel(inputs_ref, gain_ref, hidden_ref):
    z_index, y_index = lax.axis_index("z"), lax.axis_index("y")
    values = inputs_ref[...].astype(F32)
    factor = lax.rsqrt(jnp.mean(values * values, axis=-1, keepdims=True) + 1e-05)
    for k in range(NY):
        for p, z_step in enumerate(ORDER):
            columns = pl.ds(block_column(z_index, y_index, k, z_step), HD)
            block = inputs_ref[:, columns].astype(F32) * factor * gain_ref[:, columns]
            hidden_ref[k, :, p * HD : (p + 1) * HD] = block.astype(BF16)


def attention_back(packed_of, grads_of):
    factor = 1.0 / math.sqrt(HD)
    queries = jnp.concatenate([packed_of(h) for h in range(QH)], axis=0)
    grads = jnp.concatenate([grads_of(h) for h in range(QH)], axis=0)
    keys, values = packed_of(QH), packed_of(QH + 1)
    length = keys.shape[0]
    scores = dot_nt(queries, keys) * factor
    rows = lax.broadcasted_iota(jnp.int32, scores.shape, 0) % length
    cols = lax.broadcasted_iota(jnp.int32, scores.shape, 1)
    scores = jnp.where(cols <= rows, scores, -1000000000.0)
    top = jnp.max(scores, axis=-1, keepdims=True)
    raised = jnp.exp(scores - top)
    weights = raised / jnp.sum(raised, axis=-1, keepdims=True)
    grad_weights = dot_nt(grads, values)
    inner = jnp.sum(grad_weights * weights, axis=-1, keepdims=True)
    grad_scores = (weights * (grad_weights - inner) * factor).astype(BF16)
    grad_queries = dot_nn(grad_scores, keys)
    heads = [grad_queries[h * length : (h + 1) * length] for h in range(QH)]
    return heads + [dot_tn(grad_scores, queries), dot_tn(weights.astype(BF16), grads)]


def whole_block(halves):
    return jnp.concatenate([ref[...] if at is None else ref[at] for ref, at in halves], axis=0)


def pairs_of(layout, refs):
    blocks = [[(refs[i], at) for i, at in halves] for halves in layout]
    for p in range(0, len(blocks), 2):
        yield p, functools.partial(
            lambda a, b: jnp.concatenate([whole_block(a), whole_block(b)], axis=1), blocks[p], blocks[p + 1]
        )


def upper_kernel(layouts, hidden_ref, grad_ref, *refs):
    *pieces, packed_acc, grad_packed_ref, back_ref = refs[:-3] + (refs[-1], refs[-3], refs[-2])
    x_index = lax.axis_index("tensor")
    length = grad_ref.shape[0]
    chunk = length // NX
    first = True
    for k, layout in enumerate(layouts):
        for p, pair in pairs_of(layout, pieces):
            term = dot_nt(hidden_ref[k, :, p * HD : (p + 2) * HD], pair())
            packed_acc[...] = term if first else packed_acc[...] + term
            first = False
    columns = attention_back(
        lambda h: packed_acc[:, h * HD : (h + 1) * HD].astype(BF16),
        lambda h: grad_ref[:, h * HD : (h + 1) * HD],
    )
    for h, column in enumerate(columns):
        grad_packed_ref[:, h * HD : (h + 1) * HD] = column.astype(BF16)
    for k, layout in enumerate(layouts):
        for p, pair in pairs_of(layout, pieces):
            term = dot_nn(grad_packed_ref[...], pair()).astype(BF16)
            start = (k * NZ + p) * HD
            for c in range(NX):
                back_ref[(c - x_index + NX) % NX, :, start : start + 2 * HD] = term[c * chunk : (c + 1) * chunk]


def slab_kernel(layout, *refs):
    hidden, pieces, out_ref = refs[:NY], refs[NY:-1], refs[-1]
    for k in range(NY):
        total = None
        for p, pair in pairs_of(layout, pieces):
            term = dot_nt(hidden[k][:, p * HD : (p + 2) * HD], pair())
            total = term if total is None else total + term
        out_ref[k] = total.astype(BF16)


def sign_kernel(*refs):
    hidden, sign_ref, out_ref = refs[:NY], refs[NY], refs[-1]
    z_index = lax.axis_index("z")
    for k in range(NY):
        total = None
        for p in range(0, NZ, 2):
            pair = jnp.concatenate([sign_ref[(z_index + ORDER[q]) % NZ] for q in (p, p + 1)], axis=1)
            term = dot_nt(hidden[k][:, p * HD : (p + 2) * HD], pair)
            total = term if total is None else total + term
        out_ref[k] = total.astype(BF16)


def norm_back_kernel(inputs_ref, gain_ref, cotangent_ref, own_ref, *refs):
    others, out_ref = refs[:-1], refs[-1]
    x_index = lax.axis_index("tensor")
    z_index, y_index = lax.axis_index("z"), lax.axis_index("y")
    chunk = out_ref.shape[0]
    rows = pl.ds(pl.multiple_of(x_index * chunk, chunk), chunk)
    values = inputs_ref[rows, :].astype(F32)
    width = values.shape[1]
    factor = lax.rsqrt(jnp.mean(values * values, axis=-1, keepdims=True) + 1e-05)
    grads, columns = [], []
    inner = jnp.zeros((chunk, HD), F32)
    for k in range(NY):
        for p, z_step in enumerate(ORDER):
            at = (k * NZ + p) * HD
            column = pl.ds(block_column(z_index, y_index, k, z_step), HD)
            grad = own_ref[0, :, at : at + HD].astype(F32)
            for other in others:
                grad = grad + other[:, at : at + HD].astype(F32)
            grad = grad * gain_ref[:, column]
            inner = inner + grad * (inputs_ref[rows, column].astype(F32) * factor)
            grads.append(grad)
            columns.append(column)
    mean = jnp.sum(inner, axis=-1, keepdims=True) * (1.0 / width)
    for grad, column in zip(grads, columns):
        normed = inputs_ref[rows, column].astype(F32) * factor
        kept = cotangent_ref[rows, column].astype(F32)
        out_ref[:, column] = (kept + factor * (grad - normed * mean)).astype(BF16)


def lower_kernel(count, packed_ref, weight_ref, upper_ref, *refs):
    arrived, projected, out_ref, rows_ref, mixed_ref = refs[:NX], refs[NX:-3], refs[-3], refs[-2], refs[-1]
    x_index = lax.axis_index("tensor")
    pipe_index = lax.axis_index("pipe")
    chunk = arrived[0].shape[0]
    for j in range(NX):
        place = pl.multiple_of(((x_index - j + NX) % NX) * chunk, chunk)
        rows_ref[pl.ds(place, chunk), :] = arrived[j][...]
    mixed_ref[...] = jnp.zeros_like(mixed_ref)
    depth = 512

    def step(i, _):
        at = pl.ds(pl.multiple_of(i * depth, depth), depth)
        mixed_ref[...] += dot_nn(rows_ref[:, at], weight_ref[at, :])
        return 0

    lax.fori_loop(0, rows_ref.shape[1] // depth, step, 0)
    columns = attention_back(
        lambda h: packed_ref[:, h * HD : (h + 1) * HD],
        lambda h: mixed_ref[:, h * HD : (h + 1) * HD].astype(BF16),
    )
    for h, column in enumerate(columns):
        at = slice(h * HD, (h + 1) * HD)
        lower = column.astype(BF16).astype(F32)
        kept = jnp.where(pipe_index == 1, upper_ref[:, at].astype(F32), lower)
        product = projected[0][0, :, at].astype(F32)
        for other in projected[1:]:
            product = product + other[:, at].astype(F32)
        out_ref[:, at] = jnp.sum(kept * product, axis=0, keepdims=True) * (1.0 / count)


def send_z(value, steps):
    return lax.ppermute(value, "z", [(i, (i + steps) % NZ) for i in range(NZ)])


def send_y(value, steps, pipes=(0, 1)):
    pairs = [(NY * p + i, NY * p + (i + steps) % NY) for p in pipes for i in range(NY)]
    return lax.ppermute(value, ("pipe", "y"), pairs)


def send_x_upper(value, steps):
    pairs = [(NX + i, NX + (i + steps) % NX) for i in range(NX)]
    return lax.ppermute(value, ("pipe", "tensor"), pairs)


def send_down(value, steps):
    return lax.ppermute(value, ("pipe", "tensor"), [(NX + i, (i + steps) % NX) for i in range(NX)])


def local(section_input, norm_gain, cotangent, qkv_base, qkv_sign, qkv_scale, out_base):
    inputs = section_input[0]
    tokens, width = inputs.shape
    chunk = tokens // NX
    weight_out = out_base[0]
    sign = qkv_sign[0]
    rows = sign.shape[0]
    half = rows // 2
    weight = (qkv_base[0].astype(F32) + qkv_scale[0][:, None] * sign.astype(F32)).astype(BF16)

    above, below = [weight], [weight]
    for _ in range(3):
        below.append(send_z(below[-1], 1))
        above.append(send_z(above[-1], -1))
    far_first, far_second = send_z(below[3][:half], 1), send_z(above[3][half:], -1)
    sign_slab = lax.all_gather(sign, "z", axis=0, tiled=True).reshape(NZ, rows, -1)

    single = lambda i: [[(i, None)]]
    split = lambda i: [[(i, None), (i + 1, None)]]
    pair = lambda i: [[(i, 0)], [(i, 1)]]
    groups = [weight] + [jnp.stack([below[i], above[i]]) for i in (1, 2, 3)]
    groups += [jnp.concatenate([far_first, far_second], axis=0)]
    pieces, layouts = [], []
    sides = [[], [], [], []]
    for group in groups:
        from_below, from_above = send_y(group, 1, (1,)), send_y(group, -1, (1,))
        if group.ndim == 3:
            parts = (from_below[0], from_above[1])
        else:
            parts = (from_below[:half], from_above[half:])
        sides[0].append([group])
        sides[1].append([from_above])
        sides[2].append([send_y(parts[0], 1, (1,)), send_y(parts[1], -1, (1,))])
        sides[3].append([from_below])
    for side in sides:
        layout = []
        for arrays in side:
            at = len(pieces)
            pieces += arrays
            if len(arrays) == 1:
                layout += pair(at) if arrays[0].ndim == 3 else single(at)
            else:
                layout += split(at) if arrays[0].shape[0] == half else single(at) + single(at + 1)
        layouts.append(layout)

    hidden = call(
        norm_kernel, jax.ShapeDtypeStruct((NY, tokens, NZ * HD), BF16), (inputs, norm_gain), 10**7
    )
    hidden_slab = [hidden[0]] + [send_y(hidden[k], k) for k in range(1, NY)]
    grad_mixed = dot_nn(cotangent, weight_out).astype(BF16)

    flops = 2 * tokens * rows * width
    upper = pl.pallas_call(
        functools.partial(upper_kernel, layouts),
        out_shape=(
            jax.ShapeDtypeStruct((tokens, rows), BF16),
            jax.ShapeDtypeStruct((NX, chunk, width), BF16),
        ),
        in_specs=[VMEM] * (2 + len(pieces)),
        out_specs=(VMEM, VMEM),
        scratch_shapes=[pltpu.VMEM((tokens, rows), F32)],
        compiler_params=pltpu.CompilerParams(vmem_limit_bytes=40 * 1024 * 1024),
        cost_estimate=pl.CostEstimate(flops=2 * flops, bytes_accessed=100000, transcendentals=131072),
    )
    grad_upper, back = upper(hidden, grad_mixed, *pieces)

    own = pieces[: len(groups)]
    partial = call(
        functools.partial(slab_kernel, layouts[0]),
        jax.ShapeDtypeStruct((NY, tokens, rows), BF16),
        (*hidden_slab, *own),
        flops,
    )
    packed = partial[0].astype(F32)
    for k in range(1, NY):
        packed = packed + send_y(partial[k], -k, (0,)).astype(F32)
    packed = packed.astype(BF16)

    signed = call(
        sign_kernel, jax.ShapeDtypeStruct((NY, tokens, rows), BF16), (*hidden_slab, sign_slab), flops
    )
    projected = [signed] + [send_y(signed[k], -k) for k in range(1, NY)]

    received = [send_x_upper(back[j], j) for j in range(1, NX)]
    backward = call(
        norm_back_kernel,
        jax.ShapeDtypeStruct((chunk, width), BF16),
        (inputs, norm_gain, cotangent, back, *received),
        10**6,
    )
    arrived = [send_down(backward, j) for j in range(NX)]
    args = (packed, weight_out, grad_upper, *arrived, *projected)
    result = pl.pallas_call(
        functools.partial(lower_kernel, tokens * NZ * NY),
        out_shape=jax.ShapeDtypeStruct((1, rows), F32),
        in_specs=[VMEM] * len(args),
        out_specs=VMEM,
        scratch_shapes=[pltpu.VMEM((tokens, width), BF16), pltpu.VMEM((tokens, QH * HD), F32)],
        compiler_params=pltpu.CompilerParams(vmem_limit_bytes=40 * 1024 * 1024),
        cost_estimate=pl.CostEstimate(flops=flops, bytes_accessed=100000, transcendentals=131072),
    )(*args)
    return lax.psum(lax.psum(result, "y"), "z")


def solution(mesh):
    sizes = mesh.devices.shape
    fine = Mesh(mesh.devices.reshape(sizes[0], sizes[1], NZ, NY), ("pipe", "tensor", "z", "y"))
    dp = ("z", "y")
    placed = (
        P("pipe", dp, None),
        P("pipe", None),
        P(dp, None),
        P("pipe", "tensor", dp),
        P("pipe", "tensor", dp),
        P("pipe", "tensor"),
        P("pipe", None, "tensor"),
    )
    return jax.shard_map(
        local, mesh=fine, in_specs=placed, out_specs=P("pipe", "tensor"), check_vma=False
    )
```

```python
import functools
import math

import jax
import jax.numpy as jnp
from jax import lax
from jax.experimental import pallas as pl
from jax.experimental.pallas import tpu as pltpu
from jax.sharding import Mesh
from jax.sharding import PartitionSpec as P

HD = 128
QH = 8
NY = 4
NX = 4
NZ = 8

F32 = jnp.float32
BF16 = jnp.bfloat16
VMEM = pl.BlockSpec(memory_space=pltpu.VMEM)


def dot_nn(a, b):
    return lax.dot_general(a, b, (((1,), (0,)), ((), ())), preferred_element_type=F32)


def dot_nt(a, b):
    return lax.dot_general(a, b, (((1,), (1,)), ((), ())), preferred_element_type=F32)


def dot_tn(a, b):
    return lax.dot_general(a, b, (((0,), (0,)), ((), ())), preferred_element_type=F32)


def call(kernel, outs, args, flops, vmem=20):
    return pl.pallas_call(
        kernel,
        out_shape=outs,
        in_specs=[VMEM] * len(args),
        out_specs=jax.tree.map(lambda _: VMEM, outs),
        compiler_params=pltpu.CompilerParams(vmem_limit_bytes=vmem * 1024 * 1024),
        cost_estimate=pl.CostEstimate(flops=flops, bytes_accessed=100000, transcendentals=0),
    )(*args)


def norm_kernel(inputs_ref, gain_ref, hidden_ref):
    y_index = lax.axis_index("y")
    values = inputs_ref[...].astype(F32)
    factor = lax.rsqrt(jnp.mean(values * values, axis=-1, keepdims=True) + 1e-05)
    hidden = (values * factor * gain_ref[...]).astype(BF16)
    for y in range(NY):
        for z in range(NZ):
            block = hidden[:, (z * NY + y) * HD : (z * NY + y + 1) * HD]
            hidden_ref[(y - y_index + NY) % NY, :, z * HD : (z + 1) * HD] = block


def attention_back(packed_of, grads_of):
    factor = 1.0 / math.sqrt(HD)
    queries = jnp.concatenate([packed_of(h) for h in range(QH)], axis=0)
    grads = jnp.concatenate([grads_of(h) for h in range(QH)], axis=0)
    keys, values = packed_of(QH), packed_of(QH + 1)
    length = keys.shape[0]
    scores = dot_nt(queries, keys) * factor
    rows = lax.broadcasted_iota(jnp.int32, scores.shape, 0) % length
    cols = lax.broadcasted_iota(jnp.int32, scores.shape, 1)
    scores = jnp.where(cols <= rows, scores, -1000000000.0)
    top = jnp.max(scores, axis=-1, keepdims=True)
    raised = jnp.exp(scores - top)
    weights = raised / jnp.sum(raised, axis=-1, keepdims=True)
    grad_weights = dot_nt(grads, values)
    inner = jnp.sum(grad_weights * weights, axis=-1, keepdims=True)
    grad_scores = (weights * (grad_weights - inner) * factor).astype(BF16)
    grad_queries = dot_nn(grad_scores, keys)
    heads = [grad_queries[h * length : (h + 1) * length] for h in range(QH)]
    return heads + [dot_tn(grad_scores, queries), dot_tn(weights.astype(BF16), grads)]


def slab_product(hidden_ref, slab_ref):
    total = None
    for z in range(0, NZ, 2):
        pair = jnp.concatenate([slab_ref[z], slab_ref[z + 1]], axis=1)
        term = dot_nt(hidden_ref[:, z * HD : (z + 2) * HD], pair)
        total = term if total is None else total + term
    return total.astype(BF16)


def packed_kernel(*refs):
    hidden, slab_ref, out_ref = refs[:NY], refs[NY], refs[-1]
    for k in range(NY):
        out_ref[k] = slab_product(hidden[k], slab_ref)


def sign_kernel(*refs):
    hidden, slab_ref, out_ref = refs[:NY], refs[NY], refs[-1]
    y_index = lax.axis_index("y")
    for k in range(NY):
        out_ref[(y_index - k + NY) % NY] = slab_product(hidden[k], slab_ref)


def upper_kernel(grad_ref, *refs):
    parts, packed_ref, grad_packed_ref = refs[:-2], refs[-2], refs[-1]
    packed = parts[0][...].astype(F32)
    for part in parts[1:]:
        packed = packed + part[...].astype(F32)
    packed_ref[...] = packed.astype(BF16)
    columns = attention_back(
        lambda h: packed_ref[:, h * HD : (h + 1) * HD],
        lambda h: grad_ref[:, h * HD : (h + 1) * HD],
    )
    for h, column in enumerate(columns):
        grad_packed_ref[:, h * HD : (h + 1) * HD] = column.astype(BF16)


def back_kernel(*refs):
    rows, slab_ref, out_ref = refs[:NY], refs[NY], refs[-1]
    y_index = lax.axis_index("y")
    chunk = out_ref.shape[1]
    for k in range(NY):
        for z in range(0, NZ, 2):
            pair = jnp.concatenate([slab_ref[z], slab_ref[z + 1]], axis=1)
            term = dot_nn(rows[k][...], pair).astype(BF16)
            for c in range(NX):
                place = c * NY + (y_index - k + NY) % NY
                out_ref[place, :, z * HD : (z + 2) * HD] = term[c * chunk : (c + 1) * chunk]


def norm_back_kernel(inputs_ref, gain_ref, cotangent_ref, terms_ref, out_ref):
    x_index = lax.axis_index("tensor")
    chunk, width = out_ref.shape
    rows = pl.ds(pl.multiple_of(x_index * chunk, chunk), chunk)
    values = inputs_ref[rows, :].astype(F32)
    factor = lax.rsqrt(jnp.mean(values * values, axis=-1, keepdims=True) + 1e-05)
    normed = values * factor
    blocks = []
    for z in range(NZ):
        for y in range(NY):
            at = slice(z * HD, (z + 1) * HD)
            block = terms_ref[y, :, at].astype(F32)
            for x in range(1, NX):
                block = block + terms_ref[x * NY + y, :, at].astype(F32)
            blocks.append(block)
    grad = jnp.concatenate(blocks, axis=1) * gain_ref[...]
    mean = jnp.sum(grad * normed, axis=-1, keepdims=True) * (1.0 / width)
    out_ref[...] = (cotangent_ref[rows, :].astype(F32) + factor * (grad - normed * mean)).astype(BF16)


def lower_kernel(count, packed_ref, weight_ref, upper_ref, *refs):
    *arrived, projected_ref, out_ref, rows_ref, mixed_ref = refs
    x_index = lax.axis_index("tensor")
    pipe_index = lax.axis_index("pipe")
    chunk = arrived[0].shape[0]
    for j in range(NX):
        place = pl.multiple_of(((x_index - j + NX) % NX) * chunk, chunk)
        rows_ref[pl.ds(place, chunk), :] = arrived[j][...]
    mixed_ref[...] = jnp.zeros_like(mixed_ref)
    depth = 512

    def step(i, _):
        at = pl.ds(pl.multiple_of(i * depth, depth), depth)
        mixed_ref[...] += dot_nn(rows_ref[:, at], weight_ref[at, :])
        return 0

    lax.fori_loop(0, rows_ref.shape[1] // depth, step, 0)
    columns = attention_back(
        lambda h: packed_ref[:, h * HD : (h + 1) * HD],
        lambda h: mixed_ref[:, h * HD : (h + 1) * HD].astype(BF16),
    )
    for h, column in enumerate(columns):
        at = slice(h * HD, (h + 1) * HD)
        lower = column.astype(BF16).astype(F32)
        kept = jnp.where(pipe_index == 1, upper_ref[:, at].astype(F32), lower)
        product = projected_ref[:, at].astype(F32)
        out_ref[:, at] = jnp.sum(kept * product, axis=0, keepdims=True) * (1.0 / count)


def send_y(value, steps, pipes=(0, 1)):
    pairs = [(NY * p + i, NY * p + (i + steps) % NY) for p in pipes for i in range(NY)]
    return lax.ppermute(value, ("pipe", "y"), pairs)


def send_down(value, steps):
    return lax.ppermute(value, ("pipe", "tensor"), [(NX + i, (i + steps) % NX) for i in range(NX)])


def local(section_input, norm_gain, cotangent, qkv_base, qkv_sign, qkv_scale, out_base):
    inputs = section_input[0]
    tokens, width = inputs.shape
    chunk = tokens // NX
    weight_out = out_base[0]
    sign = qkv_sign[0]
    rows = sign.shape[0]
    weight = (qkv_base[0].astype(F32) + qkv_scale[0][:, None] * sign.astype(F32)).astype(BF16)
    weight_slab = lax.all_gather(weight, "z", axis=0, tiled=False)
    sign_slab = lax.all_gather(sign, "z", axis=0, tiled=False)

    hidden = call(
        norm_kernel, jax.ShapeDtypeStruct((NY, tokens, NZ * HD), BF16), (inputs, norm_gain), 10**7
    )
    hidden_slab = [hidden[0]] + [send_y(hidden[k], k) for k in range(1, NY)]
    grad_mixed = dot_nn(cotangent, weight_out).astype(BF16)

    flops = 2 * tokens * rows * width
    by_y = jax.ShapeDtypeStruct((NY, tokens, rows), BF16)
    packed_rows = jax.ShapeDtypeStruct((tokens, rows), BF16)
    partial = call(packed_kernel, by_y, (*hidden_slab, weight_slab), flops)
    parts = [partial[0]] + [send_y(partial[k], -k) for k in range(1, NY)]
    packed, grad_upper = call(upper_kernel, (packed_rows, packed_rows), (grad_mixed, *parts), 10**8)

    signed = call(sign_kernel, by_y, (*hidden_slab, sign_slab), flops)
    projected = lax.psum_scatter(signed, "y", scatter_dimension=0)

    slab_rows = [grad_upper] + [send_y(grad_upper, k, (1,)) for k in range(1, NY)]
    back = call(
        back_kernel,
        jax.ShapeDtypeStruct((NX * NY, chunk, NZ * HD), BF16),
        (*slab_rows, weight_slab),
        flops,
    )
    terms = lax.all_to_all(back, ("tensor", "y"), 0, 0)
    backward = call(
        norm_back_kernel,
        jax.ShapeDtypeStruct((chunk, width), BF16),
        (inputs, norm_gain, cotangent, terms),
        10**6,
    )
    arrived = [send_down(backward, j) for j in range(NX)]
    args = (packed, weight_out, grad_upper, *arrived, projected)
    result = pl.pallas_call(
        functools.partial(lower_kernel, tokens * NZ * NY),
        out_shape=jax.ShapeDtypeStruct((1, rows), F32),
        in_specs=[VMEM] * len(args),
        out_specs=VMEM,
        scratch_shapes=[pltpu.VMEM((tokens, width), BF16), pltpu.VMEM((tokens, QH * HD), F32)],
        compiler_params=pltpu.CompilerParams(vmem_limit_bytes=28 * 1024 * 1024),
        cost_estimate=pl.CostEstimate(flops=flops, bytes_accessed=100000, transcendentals=131072),
    )(*args)
    return lax.psum(lax.psum(result, "y"), "z")


def solution(mesh):
    sizes = mesh.devices.shape
    fine = Mesh(mesh.devices.reshape(sizes[0], sizes[1], NZ, NY), ("pipe", "tensor", "z", "y"))
    dp = ("z", "y")
    placed = (
        P("pipe", dp, None),
        P("pipe", None),
        P(dp, None),
        P("pipe", "tensor", dp),
        P("pipe", "tensor", dp),
        P("pipe", "tensor"),
        P("pipe", None, "tensor"),
    )
    return jax.shard_map(
        local, mesh=fine, in_specs=placed, out_specs=P("pipe", "tensor"), check_vma=False
    )
```

```python
import functools
import math

import jax
import jax.numpy as jnp
from jax import lax
from jax.experimental import pallas as pl
from jax.experimental.pallas import tpu as pltpu
from jax.sharding import Mesh
from jax.sharding import PartitionSpec as P

HD = 128
QH = 8
NY = 4
NX = 4
NZ = 8

F32 = jnp.float32
BF16 = jnp.bfloat16
VMEM = pl.BlockSpec(memory_space=pltpu.VMEM)
HBM = pl.BlockSpec(memory_space=pltpu.HBM)
ANY = pl.BlockSpec(memory_space=pl.ANY)


def dot_nn(a, b):
    return lax.dot_general(a, b, (((1,), (0,)), ((), ())), preferred_element_type=F32)


def dot_nt(a, b):
    return lax.dot_general(a, b, (((1,), (1,)), ((), ())), preferred_element_type=F32)


def dot_tn(a, b):
    return lax.dot_general(a, b, (((0,), (0,)), ((), ())), preferred_element_type=F32)


def call(kernel, outs, args, flops, vmem=14, unread=0, scratch=(), far=()):
    return pl.pallas_call(
        kernel,
        out_shape=outs,
        in_specs=[HBM if i in far else VMEM for i in range(len(args) - unread)] + [ANY] * unread,
        out_specs=jax.tree.map(lambda _: VMEM, outs),
        scratch_shapes=scratch,
        compiler_params=pltpu.CompilerParams(vmem_limit_bytes=vmem * 1024 * 1024),
        cost_estimate=pl.CostEstimate(flops=flops, bytes_accessed=100000, transcendentals=0),
    )(*args)


def norm_kernel(inputs_ref, gain_ref, *refs):
    turned_ref = refs[-1]
    y_index = lax.axis_index("y")
    values = inputs_ref[...].astype(F32)
    factor = lax.rsqrt(jnp.mean(values * values, axis=-1, keepdims=True) + 1e-05)
    hidden = (values * factor * gain_ref[...]).astype(BF16)
    for y in range(NY):
        for z in range(NZ):
            block = hidden[:, (z * NY + y) * HD : (z * NY + y + 1) * HD]
            turned_ref[(y - y_index + NY) % NY, :, z * HD : (z + 1) * HD] = block
    for k in range(NY):
        refs[k][...] = turned_ref[k]


def attention_back(packed_of, grads_of):
    factor = 1.0 / math.sqrt(HD)
    queries = jnp.concatenate([packed_of(h) for h in range(QH)], axis=0)
    grads = jnp.concatenate([grads_of(h) for h in range(QH)], axis=0)
    keys, values = packed_of(QH), packed_of(QH + 1)
    length = keys.shape[0]
    scores = dot_nt(queries, keys) * factor
    rows = lax.broadcasted_iota(jnp.int32, scores.shape, 0) % length
    cols = lax.broadcasted_iota(jnp.int32, scores.shape, 1)
    scores = jnp.where(cols <= rows, scores, -1000000000.0)
    top = jnp.max(scores, axis=-1, keepdims=True)
    raised = jnp.exp(scores - top)
    weights = raised / jnp.sum(raised, axis=-1, keepdims=True)
    grad_weights = dot_nt(grads, values)
    inner = jnp.sum(grad_weights * weights, axis=-1, keepdims=True)
    grad_scores = (weights * (grad_weights - inner) * factor).astype(BF16)
    grad_queries = dot_nn(grad_scores, keys)
    heads = [grad_queries[h * length : (h + 1) * length] for h in range(QH)]
    return heads + [dot_tn(grad_scores, queries), dot_tn(weights.astype(BF16), grads)]


def slab_products(hidden, slab_ref, held_ref, sems):
    copies = [
        pltpu.make_async_copy(slab_ref.at[pl.ds(z, 2)], held_ref.at[pl.ds(z, 2)], sems.at[z // 2])
        for z in range(0, NZ, 2)
    ]
    for copy in copies:
        copy.start()
    for k in range(NY):
        total = None
        for z in range(0, NZ, 2):
            if k == 0:
                copies[z // 2].wait()
            pair = jnp.concatenate([held_ref[z], held_ref[z + 1]], axis=1)
            term = dot_nt(hidden[k][:, z * HD : (z + 2) * HD], pair)
            total = term if total is None else total + term
        yield k, total


def packed_kernel(*refs):
    hidden, slab_ref, outs, (held_ref, sems) = refs[:NY], refs[NY], refs[NY + 1 : -2], refs[-2:]
    for k, total in slab_products(hidden, slab_ref, held_ref, sems):
        outs[k][...] = total.astype(BF16)


def sign_kernel(*refs):
    hidden, slab_ref, rows = refs[:NY], refs[NY], refs[NY + 1 : 2 * NY + 1]
    *outs, upper_ref, held_ref, sems = refs[2 * NY + 2 :]
    upper = None
    for k, total in slab_products(hidden, slab_ref, held_ref, sems):
        outs[k][...] = total.astype(BF16)
        term = jnp.sum(rows[k][...].astype(F32) * total, axis=0, keepdims=True)
        upper = term if upper is None else upper + term
    upper_ref[...] = upper


def summed(parts, h):
    at = slice(h * HD, (h + 1) * HD)
    total = parts[0][:, at].astype(F32)
    for part in parts[1:]:
        total = total + part[:, at].astype(F32)
    return total.astype(BF16)


def upper_kernel(grad_ref, *refs):
    parts, grad_packed_ref = refs[:-1], refs[-1]
    columns = attention_back(
        lambda h: summed(parts, h),
        lambda h: grad_ref[:, h * HD : (h + 1) * HD],
    )
    for h, column in enumerate(columns):
        grad_packed_ref[:, h * HD : (h + 1) * HD] = column.astype(BF16)


def back_kernel(*refs):
    rows, slab_ref, out_ref = refs[:NY], refs[NY], refs[-1]
    y_index = lax.axis_index("y")
    chunk = out_ref.shape[1]
    for k in range(NY):
        for z in range(0, NZ, 2):
            pair = jnp.concatenate([slab_ref[z], slab_ref[z + 1]], axis=1)
            term = dot_nn(rows[k][...], pair).astype(BF16)
            for c in range(NX):
                place = c * NY + (y_index - k + NY) % NY
                out_ref[place, :, z * HD : (z + 2) * HD] = term[c * chunk : (c + 1) * chunk]


def norm_back_kernel(inputs_ref, gain_ref, cotangent_ref, terms_ref, *refs):
    x_index = lax.axis_index("tensor")
    out_ref = refs[-1]
    chunk, width = out_ref.shape
    rows = pl.ds(pl.multiple_of(x_index * chunk, chunk), chunk)
    values = inputs_ref[rows, :].astype(F32)
    factor = lax.rsqrt(jnp.mean(values * values, axis=-1, keepdims=True) + 1e-05)
    normed = values * factor
    blocks = []
    for z in range(NZ):
        for y in range(NY):
            at = slice(z * HD, (z + 1) * HD)
            block = terms_ref[y, :, at].astype(F32)
            for x in range(1, NX):
                block = block + terms_ref[x * NY + y, :, at].astype(F32)
            blocks.append(block)
    grad = jnp.concatenate(blocks, axis=1) * gain_ref[...]
    mean = jnp.sum(grad * normed, axis=-1, keepdims=True) * (1.0 / width)
    out_ref[...] = (cotangent_ref[rows, :].astype(F32) + factor * (grad - normed * mean)).astype(BF16)


def lower_kernel(count, *refs):
    parts, arrived, projected = refs[:NY], refs[NY : NY + NX], refs[NY + NX : 2 * NY + NX]
    upper_ref, weight_ref, out_ref, rows_ref, mixed_ref, held_ref, sems = refs[2 * NY + NX :]
    x_index = lax.axis_index("tensor")
    pipe_index = lax.axis_index("pipe")
    chunk = arrived[0].shape[0]
    depth = held_ref.shape[1]
    steps = held_ref.shape[0]
    copies = [
        pltpu.make_async_copy(weight_ref.at[pl.ds(i * depth, depth)], held_ref.at[i], sems.at[i])
        for i in range(steps)
    ]
    for copy in copies:
        copy.start()
    for j in range(NX):
        place = pl.multiple_of(((x_index - j + NX) % NX) * chunk, chunk)
        rows_ref[pl.ds(place, chunk), :] = arrived[j][...]
    for i, copy in enumerate(copies):
        copy.wait()
        term = dot_nn(rows_ref[:, i * depth : (i + 1) * depth], held_ref[i])
        mixed_ref[...] = term if i == 0 else mixed_ref[...] + term
    columns = attention_back(
        lambda h: summed(parts, h),
        lambda h: mixed_ref[:, h * HD : (h + 1) * HD].astype(BF16),
    )
    for h, column in enumerate(columns):
        at = slice(h * HD, (h + 1) * HD)
        product = projected[0][:, at].astype(F32)
        for other in projected[1:]:
            product = product + other[:, at].astype(F32)
        lower = jnp.sum(column.astype(BF16).astype(F32) * product, axis=0, keepdims=True)
        out_ref[:, at] = jnp.where(pipe_index == 1, upper_ref[:, at], lower) * (1.0 / count)


def send_y(value, steps, pipes=(0, 1)):
    pairs = [(NY * p + i, NY * p + (i + steps) % NY) for p in pipes for i in range(NY)]
    return lax.ppermute(value, ("pipe", "y"), pairs)


def send_down(value, steps):
    return lax.ppermute(value, ("pipe", "tensor"), [(NX + i, (i + steps) % NX) for i in range(NX)])


def local(section_input, norm_gain, cotangent, qkv_base, qkv_sign, qkv_scale, out_base):
    inputs = section_input[0]
    tokens, width = inputs.shape
    chunk = tokens // NX
    weight_out = out_base[0]
    sign = qkv_sign[0]
    rows = sign.shape[0]
    weight = (qkv_base[0].astype(F32) + qkv_scale[0][:, None] * sign.astype(F32)).astype(BF16)
    weight_slab = lax.all_gather(weight, "z", axis=0, tiled=False)

    slab = jax.ShapeDtypeStruct((tokens, NZ * HD), BF16)
    hidden = call(norm_kernel, (slab,) * NY, (inputs, norm_gain), 10**7, scratch=[pltpu.VMEM((NY, *slab.shape), BF16)])
    hidden_slab = [hidden[0]] + [send_y(hidden[k], k) for k in range(1, NY)]
    later_sign = lax.optimization_barrier((sign, weight_slab, *hidden_slab))[0]
    sign_slab = lax.all_gather(later_sign, "z", axis=0, tiled=False)
    grad_mixed = dot_nn(cotangent, weight_out).astype(BF16)

    flops = 2 * tokens * rows * width
    slab_scratch = [pltpu.VMEM((NZ, rows, HD), BF16), pltpu.SemaphoreType.DMA((NZ // 2,))]
    packed_rows = jax.ShapeDtypeStruct((tokens, rows), BF16)
    partial = call(
        packed_kernel, (packed_rows,) * NY, (*hidden_slab, weight_slab), flops, scratch=slab_scratch, far=(NY,), vmem=60
    )
    parts = [partial[0]] + [send_y(partial[k], -k, (1,)) for k in range(1, NY)]
    grad_upper = call(upper_kernel, packed_rows, (grad_mixed, *parts), 10**8)

    slab_rows = [grad_upper] + [send_y(grad_upper, k, (1,)) for k in range(1, NY)]
    later = lax.optimization_barrier((*partial, grad_upper))
    parts = [partial[0]] + [send_y(later[k], -k, (0,)) for k in range(1, NY)]
    back = call(
        back_kernel,
        jax.ShapeDtypeStruct((NX * NY, chunk, NZ * HD), BF16),
        (*slab_rows, weight_slab),
        flops,
    )
    *signed, upper_total = call(
        sign_kernel,
        (packed_rows,) * NY + (jax.ShapeDtypeStruct((1, rows), F32),),
        (*hidden_slab, sign_slab, *slab_rows, back),
        flops,
        unread=1,
        scratch=slab_scratch,
        far=(NY,),
        vmem=44,
    )
    projected = [signed[0]] + [send_y(signed[k], -k, (0,)) for k in range(1, NY)]
    terms = lax.all_to_all(back, ("tensor", "y"), 0, 0)
    backward = call(
        norm_back_kernel,
        jax.ShapeDtypeStruct((chunk, width), BF16),
        (inputs, norm_gain, cotangent, terms, upper_total, *parts[1:]),
        10**6,
        unread=NY,
    )
    arrived = [send_down(backward, j) for j in range(NX)]
    args = (*parts, *arrived, *projected, upper_total, weight_out)
    depth = width // 8
    result = pl.pallas_call(
        functools.partial(lower_kernel, tokens * NZ * NY),
        out_shape=jax.ShapeDtypeStruct((1, rows), F32),
        in_specs=[VMEM] * (len(args) - 1) + [HBM],
        out_specs=VMEM,
        scratch_shapes=[
            pltpu.VMEM((tokens, width), BF16),
            pltpu.VMEM((tokens, QH * HD), F32),
            pltpu.VMEM((8, depth, QH * HD), BF16),
            pltpu.SemaphoreType.DMA((8,)),
        ],
        compiler_params=pltpu.CompilerParams(vmem_limit_bytes=56 * 1024 * 1024),
        cost_estimate=pl.CostEstimate(flops=flops, bytes_accessed=100000, transcendentals=131072),
    )(*args)
    return lax.psum(lax.psum(result, "y"), "z")


def solution(mesh):
    sizes = mesh.devices.shape
    fine = Mesh(mesh.devices.reshape(sizes[0], sizes[1], NZ, NY), ("pipe", "tensor", "z", "y"))
    dp = ("z", "y")
    placed = (
        P("pipe", dp, None),
        P("pipe", None),
        P(dp, None),
        P("pipe", "tensor", dp),
        P("pipe", "tensor", dp),
        P("pipe", "tensor"),
        P("pipe", None, "tensor"),
    )
    return jax.shard_map(
        local, mesh=fine, in_specs=placed, out_specs=P("pipe", "tensor"), check_vma=False
    )
```

```python
import functools
import math

import jax
import jax.numpy as jnp
from jax import lax
from jax.experimental import pallas as pl
from jax.experimental.pallas import tpu as pltpu
from jax.sharding import Mesh
from jax.sharding import PartitionSpec as P

HD = 128
QH = 8
NY = 4
NX = 4
NZ = 8

F32 = jnp.float32
BF16 = jnp.bfloat16
VMEM = pl.BlockSpec(memory_space=pltpu.VMEM)
ANY = pl.BlockSpec(memory_space=pl.ANY)


def dot_nn(a, b):
    return lax.dot_general(a, b, (((1,), (0,)), ((), ())), preferred_element_type=F32)


def dot_nt(a, b):
    return lax.dot_general(a, b, (((1,), (1,)), ((), ())), preferred_element_type=F32)


def dot_tn(a, b):
    return lax.dot_general(a, b, (((0,), (0,)), ((), ())), preferred_element_type=F32)


def call(kernel, outs, args, flops, vmem=14, unread=0, scratch=()):
    return pl.pallas_call(
        kernel,
        out_shape=outs,
        in_specs=[VMEM] * (len(args) - unread) + [ANY] * unread,
        out_specs=jax.tree.map(lambda _: VMEM, outs),
        scratch_shapes=scratch,
        compiler_params=pltpu.CompilerParams(vmem_limit_bytes=vmem * 1024 * 1024),
        cost_estimate=pl.CostEstimate(flops=flops, bytes_accessed=100000, transcendentals=0),
    )(*args)


def norm_kernel(inputs_ref, gain_ref, *refs):
    turned_ref = refs[-1]
    y_index = lax.axis_index("y")
    values = inputs_ref[...].astype(F32)
    factor = lax.rsqrt(jnp.mean(values * values, axis=-1, keepdims=True) + 1e-05)
    hidden = (values * factor * gain_ref[...]).astype(BF16)
    for y in range(NY):
        for z in range(NZ):
            block = hidden[:, (z * NY + y) * HD : (z * NY + y + 1) * HD]
            turned_ref[(y - y_index + NY) % NY, :, z * HD : (z + 1) * HD] = block
    for k in range(NY):
        refs[k][...] = turned_ref[k]


def attention_back(packed_of, grads_of):
    factor = 1.0 / math.sqrt(HD)
    queries = jnp.concatenate([packed_of(h) for h in range(QH)], axis=0)
    grads = jnp.concatenate([grads_of(h) for h in range(QH)], axis=0)
    keys, values = packed_of(QH), packed_of(QH + 1)
    length = keys.shape[0]
    scores = dot_nt(queries, keys) * factor
    rows = lax.broadcasted_iota(jnp.int32, scores.shape, 0) % length
    cols = lax.broadcasted_iota(jnp.int32, scores.shape, 1)
    scores = jnp.where(cols <= rows, scores, -1000000000.0)
    top = jnp.max(scores, axis=-1, keepdims=True)
    raised = jnp.exp(scores - top)
    weights = raised / jnp.sum(raised, axis=-1, keepdims=True)
    grad_weights = dot_nt(grads, values)
    inner = jnp.sum(grad_weights * weights, axis=-1, keepdims=True)
    grad_scores = (weights * (grad_weights - inner) * factor).astype(BF16)
    grad_queries = dot_nn(grad_scores, keys)
    heads = [grad_queries[h * length : (h + 1) * length] for h in range(QH)]
    return heads + [dot_tn(grad_scores, queries), dot_tn(weights.astype(BF16), grads)]


def slab_kernel(*refs):
    hidden, slab_ref, outs, done_ref = refs[:NY], refs[NY], refs[-NY - 1 : -1], refs[-1]
    done_ref[...] = jnp.zeros_like(done_ref)
    for k in range(NY):
        total = None
        for z in range(0, NZ, 2):
            pair = jnp.concatenate([slab_ref[z], slab_ref[z + 1]], axis=1)
            term = dot_nt(hidden[k][:, z * HD : (z + 2) * HD], pair)
            total = term if total is None else total + term
        outs[k][...] = total.astype(BF16)


def summed(parts, h):
    at = slice(h * HD, (h + 1) * HD)
    total = parts[0][:, at].astype(F32)
    for part in parts[1:]:
        total = total + part[:, at].astype(F32)
    return total.astype(BF16)


def upper_kernel(grad_ref, *refs):
    parts, grad_packed_ref = refs[:-1], refs[-1]
    columns = attention_back(
        lambda h: summed(parts, h),
        lambda h: grad_ref[:, h * HD : (h + 1) * HD],
    )
    for h, column in enumerate(columns):
        grad_packed_ref[:, h * HD : (h + 1) * HD] = column.astype(BF16)


def back_kernel(*refs):
    rows, slab_ref, out_ref, done_ref = refs[:NY], refs[NY], refs[-2], refs[-1]
    done_ref[...] = jnp.zeros_like(done_ref)
    y_index = lax.axis_index("y")
    chunk = out_ref.shape[1]
    for k in range(NY):
        for z in range(0, NZ, 2):
            pair = jnp.concatenate([slab_ref[z], slab_ref[z + 1]], axis=1)
            term = dot_nn(rows[k][...], pair).astype(BF16)
            for c in range(NX):
                place = c * NY + (y_index - k + NY) % NY
                out_ref[place, :, z * HD : (z + 2) * HD] = term[c * chunk : (c + 1) * chunk]


def norm_back_kernel(inputs_ref, gain_ref, cotangent_ref, terms_ref, *refs):
    x_index = lax.axis_index("tensor")
    out_ref = refs[-1]
    chunk, width = out_ref.shape
    rows = pl.ds(pl.multiple_of(x_index * chunk, chunk), chunk)
    values = inputs_ref[rows, :].astype(F32)
    factor = lax.rsqrt(jnp.mean(values * values, axis=-1, keepdims=True) + 1e-05)
    normed = values * factor
    blocks = []
    for z in range(NZ):
        for y in range(NY):
            at = slice(z * HD, (z + 1) * HD)
            block = terms_ref[y, :, at].astype(F32)
            for x in range(1, NX):
                block = block + terms_ref[x * NY + y, :, at].astype(F32)
            blocks.append(block)
    grad = jnp.concatenate(blocks, axis=1) * gain_ref[...]
    mean = jnp.sum(grad * normed, axis=-1, keepdims=True) * (1.0 / width)
    out_ref[...] = (cotangent_ref[rows, :].astype(F32) + factor * (grad - normed * mean)).astype(BF16)


def lower_kernel(count, mixed_ref, upper_ref, *refs):
    parts, projected, out_ref, turned_ref = refs[:NY], refs[NY:-2], refs[-2], refs[-1]
    pipe_index = lax.axis_index("pipe")
    x_index = lax.axis_index("tensor")
    chunk = turned_ref.shape[0] // NX
    for j in range(NX):
        place = pl.multiple_of(((x_index - j + NX) % NX) * chunk, chunk)
        turned_ref[pl.ds(place, chunk), :] = mixed_ref[j * chunk : (j + 1) * chunk]
    columns = attention_back(
        lambda h: summed(parts, h),
        lambda h: turned_ref[:, h * HD : (h + 1) * HD],
    )
    for h, column in enumerate(columns):
        at = slice(h * HD, (h + 1) * HD)
        lower = column.astype(BF16).astype(F32)
        kept = jnp.where(pipe_index == 1, upper_ref[:, at].astype(F32), lower)
        product = projected[0][:, at].astype(F32)
        for other in projected[1:]:
            product = product + other[:, at].astype(F32)
        out_ref[:, at] = jnp.sum(kept * product, axis=0, keepdims=True) * (1.0 / count)


def send_y(value, steps, pipes=(0, 1)):
    pairs = [(NY * p + i, NY * p + (i + steps) % NY) for p in pipes for i in range(NY)]
    return lax.ppermute(value, ("pipe", "y"), pairs)


def send_down(value, steps):
    return lax.ppermute(value, ("pipe", "tensor"), [(NX + i, (i + steps) % NX) for i in range(NX)])


def local(section_input, norm_gain, cotangent, qkv_base, qkv_sign, qkv_scale, out_base):
    inputs = section_input[0]
    tokens, width = inputs.shape
    chunk = tokens // NX
    weight_out = out_base[0]
    sign = qkv_sign[0]
    rows = sign.shape[0]
    weight = (qkv_base[0].astype(F32) + qkv_scale[0][:, None] * sign.astype(F32)).astype(BF16)
    weight_slab = lax.all_gather(weight, "z", axis=0, tiled=False)

    slab = jax.ShapeDtypeStruct((tokens, NZ * HD), BF16)
    hidden = call(norm_kernel, (slab,) * NY, (inputs, norm_gain), 10**7, scratch=[pltpu.VMEM((NY, *slab.shape), BF16)])
    hidden_slab = [hidden[0]] + [send_y(hidden[k], k) for k in range(1, NY)]
    later_sign = lax.optimization_barrier((sign, weight_slab, *hidden_slab))[0]
    sign_slab = lax.all_gather(later_sign, "z", axis=0, tiled=False)
    grad_mixed = dot_nn(cotangent, weight_out).astype(BF16)

    flops = 2 * tokens * rows * width
    packed_rows = jax.ShapeDtypeStruct((tokens, rows), BF16)
    done = jax.ShapeDtypeStruct((8, HD), F32)
    *partial, _ = call(slab_kernel, (packed_rows,) * NY + (done,), (*hidden_slab, weight_slab), flops)
    parts = [partial[0]] + [send_y(partial[k], -k) for k in range(1, NY)]
    grad_upper = call(upper_kernel, packed_rows, (grad_mixed, *parts), 10**8)
    slab_rows = [grad_upper] + [send_y(grad_upper, k) for k in range(1, NY)]
    back, after_back = call(
        back_kernel,
        (jax.ShapeDtypeStruct((NX * NY, chunk, NZ * HD), BF16), done),
        (*slab_rows, weight_slab),
        flops,
    )
    *signed, after_signed = call(
        slab_kernel, (packed_rows,) * NY + (done,), (*hidden_slab, sign_slab, after_back), flops, unread=1
    )
    projected = [signed[0]] + [send_y(signed[k], -k) for k in range(1, NY)]
    terms = lax.all_to_all(back, ("tensor", "y"), 0, 0)
    backward = call(
        norm_back_kernel,
        jax.ShapeDtypeStruct((chunk, width), BF16),
        (inputs, norm_gain, cotangent, terms, after_signed),
        10**6,
        unread=1,
    )
    arrived = [send_down(backward, j) for j in range(NX)]
    grad_mixed_lower = dot_nn(jnp.concatenate(arrived, axis=0), weight_out).astype(BF16)
    partial_sum = call(
        functools.partial(lower_kernel, tokens * NZ * NY),
        jax.ShapeDtypeStruct((1, rows), F32),
        (grad_mixed_lower, grad_upper, *parts, *projected),
        10**8,
        scratch=[pltpu.VMEM((tokens, QH * HD), BF16)],
    )
    copies = jnp.broadcast_to(partial_sum, (NZ * NY, rows))
    return jnp.sum(lax.all_to_all(copies, ("z", "y"), 0, 0), axis=0, keepdims=True)


def solution(mesh):
    sizes = mesh.devices.shape
    fine = Mesh(mesh.devices.reshape(sizes[0], sizes[1], NZ, NY), ("pipe", "tensor", "z", "y"))
    dp = ("z", "y")
    placed = (
        P("pipe", dp, None),
        P("pipe", None),
        P(dp, None),
        P("pipe", "tensor", dp),
        P("pipe", "tensor", dp),
        P("pipe", "tensor"),
        P("pipe", None, "tensor"),
    )
    return jax.shard_map(
        local, mesh=fine, in_specs=placed, out_specs=P("pipe", "tensor"), check_vma=False
    )
```

```python
import functools
import math

import jax
import jax.numpy as jnp
from jax import lax
from jax.experimental import pallas as pl
from jax.experimental.pallas import tpu as pltpu
from jax.sharding import Mesh
from jax.sharding import PartitionSpec as P

HD = 128
QH = 8
NY = 4
NX = 4
NZ = 8

F32 = jnp.float32
BF16 = jnp.bfloat16
VMEM = pl.BlockSpec(memory_space=pltpu.VMEM)
ANY = pl.BlockSpec(memory_space=pl.ANY)


def dot_nn(a, b):
    return lax.dot_general(a, b, (((1,), (0,)), ((), ())), preferred_element_type=F32)


def dot_nt(a, b):
    return lax.dot_general(a, b, (((1,), (1,)), ((), ())), preferred_element_type=F32)


def dot_tn(a, b):
    return lax.dot_general(a, b, (((0,), (0,)), ((), ())), preferred_element_type=F32)


def call(kernel, outs, args, flops, vmem=14, unread=0, scratch=()):
    return pl.pallas_call(
        kernel,
        out_shape=outs,
        in_specs=[VMEM] * (len(args) - unread) + [ANY] * unread,
        out_specs=jax.tree.map(lambda _: VMEM, outs),
        scratch_shapes=scratch,
        compiler_params=pltpu.CompilerParams(vmem_limit_bytes=vmem * 1024 * 1024),
        cost_estimate=pl.CostEstimate(flops=flops, bytes_accessed=100000, transcendentals=0),
    )(*args)


def norm_kernel(inputs_ref, gain_ref, *refs):
    quarter_ref, turned_ref = refs[-2:]
    quarter_ref[...] = quarter(inputs_ref)
    y_index = lax.axis_index("y")
    values = inputs_ref[...].astype(F32)
    factor = lax.rsqrt(jnp.mean(values * values, axis=-1, keepdims=True) + 1e-05)
    hidden = (values * factor * gain_ref[...]).astype(BF16)
    for y in range(NY):
        for z in range(NZ):
            block = hidden[:, (z * NY + y) * HD : (z * NY + y + 1) * HD]
            turned_ref[(y - y_index + NY) % NY, :, z * HD : (z + 1) * HD] = block
    for k in range(NY):
        refs[k][...] = turned_ref[k]


def attention_back(packed_of, grads_of):
    factor = 1.0 / math.sqrt(HD)
    queries = jnp.concatenate([packed_of(h) for h in range(QH)], axis=0)
    grads = jnp.concatenate([grads_of(h) for h in range(QH)], axis=0)
    keys, values = packed_of(QH), packed_of(QH + 1)
    length = keys.shape[0]
    scores = dot_nt(queries, keys) * factor
    rows = lax.broadcasted_iota(jnp.int32, scores.shape, 0) % length
    cols = lax.broadcasted_iota(jnp.int32, scores.shape, 1)
    scores = jnp.where(cols <= rows, scores, -1000000000.0)
    top = jnp.max(scores, axis=-1, keepdims=True)
    raised = jnp.exp(scores - top)
    weights = raised / jnp.sum(raised, axis=-1, keepdims=True)
    grad_weights = dot_nt(grads, values)
    inner = jnp.sum(grad_weights * weights, axis=-1, keepdims=True)
    grad_scores = (weights * (grad_weights - inner) * factor).astype(BF16)
    grad_queries = dot_nn(grad_scores, keys)
    heads = [grad_queries[h * length : (h + 1) * length] for h in range(QH)]
    return heads + [dot_tn(grad_scores, queries), dot_tn(weights.astype(BF16), grads)]


def slab_products(hidden, slab_ref):
    for k in range(NY):
        total = None
        for z in range(0, NZ, 2):
            pair = jnp.concatenate([slab_ref[z], slab_ref[z + 1]], axis=1)
            term = dot_nt(hidden[k][:, z * HD : (z + 2) * HD], pair)
            total = term if total is None else total + term
        yield k, total.astype(BF16)


def packed_kernel(*refs):
    for k, product in slab_products(refs[:NY], refs[NY]):
        refs[NY + 1 + k][...] = product


def sign_kernel(*refs):
    out_ref, done_ref = refs[-2:]
    done_ref[...] = jnp.zeros_like(done_ref)
    y_index = lax.axis_index("y")
    for k, product in slab_products(refs[:NY], refs[NY]):
        out_ref[(y_index - k + NY) % NY] = product


def summed(parts, h):
    at = slice(h * HD, (h + 1) * HD)
    total = parts[0][:, at].astype(F32)
    for part in parts[1:]:
        total = total + part[:, at].astype(F32)
    return total.astype(BF16)


def upper_kernel(grad_ref, *refs):
    parts, grad_packed_ref = refs[:-1], refs[-1]
    columns = attention_back(
        lambda h: summed(parts, h),
        lambda h: grad_ref[:, h * HD : (h + 1) * HD],
    )
    for h, column in enumerate(columns):
        grad_packed_ref[:, h * HD : (h + 1) * HD] = column.astype(BF16)


def back_kernel(*refs):
    rows, slab_ref, out_ref, done_ref = refs[:NY], refs[NY], refs[-2], refs[-1]
    done_ref[...] = jnp.zeros_like(done_ref)
    y_index = lax.axis_index("y")
    chunk = out_ref.shape[1]
    for k in range(NY):
        for z in range(0, NZ, 2):
            pair = jnp.concatenate([slab_ref[z], slab_ref[z + 1]], axis=1)
            term = dot_nn(rows[k][...], pair).astype(BF16)
            for c in range(NX):
                place = c * NY + (y_index - k + NY) % NY
                out_ref[place, :, z * HD : (z + 2) * HD] = term[c * chunk : (c + 1) * chunk]


def norm_back_kernel(inputs_ref, gain_ref, cotangent_ref, terms_ref, *refs):
    out_ref = refs[-1]
    width = out_ref.shape[1]
    values = inputs_ref[...].astype(F32)
    factor = lax.rsqrt(jnp.mean(values * values, axis=-1, keepdims=True) + 1e-05)
    normed = values * factor
    blocks = []
    for z in range(NZ):
        for y in range(NY):
            at = slice(z * HD, (z + 1) * HD)
            block = terms_ref[y, :, at].astype(F32)
            for x in range(1, NX):
                block = block + terms_ref[x * NY + y, :, at].astype(F32)
            blocks.append(block)
    grad = jnp.concatenate(blocks, axis=1) * gain_ref[...]
    mean = jnp.sum(grad * normed, axis=-1, keepdims=True) * (1.0 / width)
    out_ref[...] = (cotangent_ref[...].astype(F32) + factor * (grad - normed * mean)).astype(BF16)


def quarter(ref):
    chunk = ref.shape[0] // NX
    return ref[pl.ds(pl.multiple_of(lax.axis_index("tensor") * chunk, chunk), chunk), :]


def mixed_kernel(rows_ref, weight_ref, out_ref, quarter_ref, total_ref):
    depth = 512
    quarter_ref[...] = quarter(rows_ref)
    total_ref[...] = jnp.zeros_like(total_ref)

    def step(i, _):
        at = pl.ds(pl.multiple_of(i * depth, depth), depth)
        total_ref[...] += dot_nn(rows_ref[:, at], weight_ref[at, :])
        return 0

    lax.fori_loop(0, weight_ref.shape[0] // depth, step, 0)
    out_ref[...] = total_ref[...].astype(BF16)


def lower_kernel(count, mixed_ref, upper_ref, projected_ref, *refs):
    parts, out_ref, turned_ref = refs[:NY], refs[-2], refs[-1]
    pipe_index = lax.axis_index("pipe")
    x_index = lax.axis_index("tensor")
    chunk = turned_ref.shape[0] // NX
    for j in range(NX):
        place = pl.multiple_of(((x_index - j + NX) % NX) * chunk, chunk)
        turned_ref[pl.ds(place, chunk), :] = mixed_ref[j * chunk : (j + 1) * chunk]
    columns = attention_back(
        lambda h: summed(parts, h),
        lambda h: turned_ref[:, h * HD : (h + 1) * HD],
    )
    for h, column in enumerate(columns):
        at = slice(h * HD, (h + 1) * HD)
        lower = column.astype(BF16).astype(F32)
        kept = jnp.where(pipe_index == 1, upper_ref[:, at].astype(F32), lower)
        product = projected_ref[:, at].astype(F32)
        out_ref[:, at] = jnp.sum(kept * product, axis=0, keepdims=True) * (1.0 / count)


def send_y(value, steps, pipes=(0, 1)):
    pairs = [(NY * p + i, NY * p + (i + steps) % NY) for p in pipes for i in range(NY)]
    return lax.ppermute(value, ("pipe", "y"), pairs)


def send_down(value, steps):
    return lax.ppermute(value, ("pipe", "tensor"), [(NX + i, (i + steps) % NX) for i in range(NX)])


def local(section_input, norm_gain, cotangent, qkv_base, qkv_sign, qkv_scale, out_base):
    inputs = section_input[0]
    tokens, width = inputs.shape
    chunk = tokens // NX
    weight_out = out_base[0]
    sign = qkv_sign[0]
    rows = sign.shape[0]
    weight = (qkv_base[0].astype(F32) + qkv_scale[0][:, None] * sign.astype(F32)).astype(BF16)
    weight_slab = lax.all_gather(weight, "z", axis=0, tiled=False)

    slab = jax.ShapeDtypeStruct((tokens, NZ * HD), BF16)
    quarter_rows = jax.ShapeDtypeStruct((chunk, width), BF16)
    *hidden, own_inputs = call(norm_kernel, (slab,) * NY + (quarter_rows,), (inputs, norm_gain), 10**7, scratch=[pltpu.VMEM((NY, *slab.shape), BF16)])
    hidden_slab = [hidden[0]] + [send_y(hidden[k], k) for k in range(1, NY)]
    later_sign = lax.optimization_barrier((sign, weight_slab, *hidden_slab))[0]
    sign_slab = lax.all_gather(later_sign, "z", axis=0, tiled=False)
    mixed_rows = jax.ShapeDtypeStruct((tokens, QH * HD), BF16)
    mixed_total = [pltpu.VMEM(mixed_rows.shape, F32)]
    grad_mixed, own_cotangent = call(mixed_kernel, (mixed_rows, quarter_rows), (cotangent, weight_out), 10**9, scratch=mixed_total)
    flops = 2 * tokens * rows * width
    packed_rows = jax.ShapeDtypeStruct((tokens, rows), BF16)
    done = jax.ShapeDtypeStruct((8, HD), F32)
    partial = call(packed_kernel, (packed_rows,) * NY, (*hidden_slab, weight_slab), flops)
    parts = [partial[0]] + [send_y(partial[k], -k) for k in (1, 3, 2)]
    grad_upper = call(upper_kernel, packed_rows, (grad_mixed, *parts), 10**8)
    near, back_near, far = (send_y(grad_upper, k) for k in (1, 3, 2))
    slab_rows = [grad_upper, near, far, back_near]
    back, after_back = call(
        back_kernel,
        (jax.ShapeDtypeStruct((NX * NY, chunk, NZ * HD), BF16), done),
        (*slab_rows, weight_slab),
        flops,
    )
    signed, after_signed = call(
        sign_kernel,
        (jax.ShapeDtypeStruct((NY, tokens, rows), BF16), done),
        (*hidden_slab, sign_slab, after_back),
        flops,
        unread=1,
    )
    projected = lax.psum_scatter(signed, "y", scatter_dimension=0)
    terms = lax.all_to_all(back, ("tensor", "y"), 0, 0)
    backward = call(
        norm_back_kernel,
        jax.ShapeDtypeStruct((chunk, width), BF16),
        (own_inputs, norm_gain, own_cotangent, terms, after_signed),
        10**11,
        unread=1,
    )
    arrived = [send_down(backward, j) for j in range(NX)]
    grad_mixed_lower = dot_nn(jnp.concatenate(arrived, axis=0), weight_out).astype(BF16)
    partial_sum = call(
        functools.partial(lower_kernel, tokens * NZ * NY),
        jax.ShapeDtypeStruct((1, rows), F32),
        (grad_mixed_lower, grad_upper, projected, *parts),
        10**8,
        scratch=[pltpu.VMEM(mixed_rows.shape, BF16)],
    )
    copies = jnp.broadcast_to(partial_sum, (NZ * NY, rows))
    return jnp.sum(lax.all_to_all(copies, ("z", "y"), 0, 0), axis=0, keepdims=True)


def solution(mesh):
    sizes = mesh.devices.shape
    fine = Mesh(mesh.devices.reshape(sizes[0], sizes[1], NZ, NY), ("pipe", "tensor", "z", "y"))
    dp = ("z", "y")
    placed = (
        P("pipe", dp, None),
        P("pipe", None),
        P(dp, None),
        P("pipe", "tensor", dp),
        P("pipe", "tensor", dp),
        P("pipe", "tensor"),
        P("pipe", None, "tensor"),
    )
    return jax.shard_map(
        local, mesh=fine, in_specs=placed, out_specs=P("pipe", "tensor"), check_vma=False
    )
```

```python
import functools
import math

import jax
import jax.numpy as jnp
from jax import lax
from jax.experimental import pallas as pl
from jax.experimental.pallas import tpu as pltpu
from jax.sharding import Mesh
from jax.sharding import PartitionSpec as P

HD = 128
QH = 8
NY = 4
NX = 4
NZ = 8

F32 = jnp.float32
BF16 = jnp.bfloat16
VMEM = pl.BlockSpec(memory_space=pltpu.VMEM)
ANY = pl.BlockSpec(memory_space=pl.ANY)


def dot_nn(a, b):
    return lax.dot_general(a, b, (((1,), (0,)), ((), ())), preferred_element_type=F32)


def dot_nt(a, b):
    return lax.dot_general(a, b, (((1,), (1,)), ((), ())), preferred_element_type=F32)


def dot_tn(a, b):
    return lax.dot_general(a, b, (((0,), (0,)), ((), ())), preferred_element_type=F32)


def call(kernel, outs, args, flops, vmem=14, unread=0, scratch=()):
    return pl.pallas_call(
        kernel,
        out_shape=outs,
        in_specs=[VMEM] * (len(args) - unread) + [ANY] * unread,
        out_specs=jax.tree.map(lambda _: VMEM, outs),
        scratch_shapes=scratch,
        compiler_params=pltpu.CompilerParams(vmem_limit_bytes=vmem * 1024 * 1024),
        cost_estimate=pl.CostEstimate(flops=flops, bytes_accessed=100000, transcendentals=0),
    )(*args)


def norm_kernel(inputs_ref, gain_ref, *refs):
    quarter_ref, turned_ref = refs[-2:]
    quarter_ref[...] = quarter(inputs_ref)
    y_index = lax.axis_index("y")
    values = inputs_ref[...].astype(F32)
    factor = lax.rsqrt(jnp.mean(values * values, axis=-1, keepdims=True) + 1e-05)
    hidden = (values * factor * gain_ref[...]).astype(BF16)
    for y in range(NY):
        for z in range(NZ):
            block = hidden[:, (z * NY + y) * HD : (z * NY + y + 1) * HD]
            turned_ref[(y - y_index + NY) % NY, :, z * HD : (z + 1) * HD] = block
    for k in range(NY):
        refs[k][...] = turned_ref[k]


def attention_back(packed_of, grads_of):
    factor = 1.0 / math.sqrt(HD)
    queries = jnp.concatenate([packed_of(h) for h in range(QH)], axis=0)
    grads = jnp.concatenate([grads_of(h) for h in range(QH)], axis=0)
    keys, values = packed_of(QH), packed_of(QH + 1)
    length = keys.shape[0]
    scores = dot_nt(queries, keys) * factor
    rows = lax.broadcasted_iota(jnp.int32, scores.shape, 0) % length
    cols = lax.broadcasted_iota(jnp.int32, scores.shape, 1)
    scores = jnp.where(cols <= rows, scores, -1000000000.0)
    top = jnp.max(scores, axis=-1, keepdims=True)
    raised = jnp.exp(scores - top)
    weights = raised / jnp.sum(raised, axis=-1, keepdims=True)
    grad_weights = dot_nt(grads, values)
    inner = jnp.sum(grad_weights * weights, axis=-1, keepdims=True)
    grad_scores = (weights * (grad_weights - inner) * factor).astype(BF16)
    grad_queries = dot_nn(grad_scores, keys)
    heads = [grad_queries[h * length : (h + 1) * length] for h in range(QH)]
    return heads + [dot_tn(grad_scores, queries), dot_tn(weights.astype(BF16), grads)]


def slab_products(hidden, slab_ref):
    for k in range(NY):
        total = None
        for z in range(0, NZ, 2):
            pair = jnp.concatenate([slab_ref[z], slab_ref[z + 1]], axis=1)
            term = dot_nt(hidden[k][:, z * HD : (z + 2) * HD], pair)
            total = term if total is None else total + term
        yield k, total.astype(BF16)


def packed_kernel(*refs):
    for k, product in slab_products(refs[:NY], refs[NY]):
        refs[NY + 1 + k][...] = product


def sign_kernel(*refs):
    hidden, slab_ref, rows = refs[:NY], refs[NY], refs[NY + 1 : 2 * NY + 1]
    out_ref, upper_ref = refs[-2:]
    y_index = lax.axis_index("y")
    upper = None
    for k, product in slab_products(hidden, slab_ref):
        out_ref[(y_index - k + NY) % NY] = product
        term = jnp.sum(rows[k][...].astype(F32) * product.astype(F32), axis=0, keepdims=True)
        upper = term if upper is None else upper + term
    upper_ref[...] = upper


def summed(parts, h):
    at = slice(h * HD, (h + 1) * HD)
    total = parts[0][:, at].astype(F32)
    for part in parts[1:]:
        total = total + part[:, at].astype(F32)
    return total.astype(BF16)


def upper_kernel(grad_ref, *refs):
    parts, grad_packed_ref = refs[:-1], refs[-1]
    columns = attention_back(
        lambda h: summed(parts, h),
        lambda h: grad_ref[:, h * HD : (h + 1) * HD],
    )
    for h, column in enumerate(columns):
        grad_packed_ref[:, h * HD : (h + 1) * HD] = column.astype(BF16)


def back_kernel(*refs):
    rows, slab_ref, out_ref = refs[:NY], refs[NY], refs[-1]
    y_index = lax.axis_index("y")
    chunk = out_ref.shape[1]
    for k in range(NY):
        for z in range(0, NZ, 2):
            pair = jnp.concatenate([slab_ref[z], slab_ref[z + 1]], axis=1)
            term = dot_nn(rows[k][...], pair).astype(BF16)
            for c in range(NX):
                place = c * NY + (y_index - k + NY) % NY
                out_ref[place, :, z * HD : (z + 2) * HD] = term[c * chunk : (c + 1) * chunk]


def norm_back_kernel(inputs_ref, gain_ref, cotangent_ref, terms_ref, out_ref):
    width = out_ref.shape[1]
    values = inputs_ref[...].astype(F32)
    factor = lax.rsqrt(jnp.mean(values * values, axis=-1, keepdims=True) + 1e-05)
    normed = values * factor
    blocks = []
    for z in range(NZ):
        for y in range(NY):
            at = slice(z * HD, (z + 1) * HD)
            block = terms_ref[y, :, at].astype(F32)
            for x in range(1, NX):
                block = block + terms_ref[x * NY + y, :, at].astype(F32)
            blocks.append(block)
    grad = jnp.concatenate(blocks, axis=1) * gain_ref[...]
    mean = jnp.sum(grad * normed, axis=-1, keepdims=True) * (1.0 / width)
    out_ref[...] = (cotangent_ref[...].astype(F32) + factor * (grad - normed * mean)).astype(BF16)


def quarter(ref):
    chunk = ref.shape[0] // NX
    return ref[pl.ds(pl.multiple_of(lax.axis_index("tensor") * chunk, chunk), chunk), :]


def mixed_kernel(rows_ref, weight_ref, out_ref, quarter_ref, total_ref):
    depth = 512
    quarter_ref[...] = quarter(rows_ref)
    total_ref[...] = jnp.zeros_like(total_ref)

    def step(i, _):
        at = pl.ds(pl.multiple_of(i * depth, depth), depth)
        total_ref[...] += dot_nn(rows_ref[:, at], weight_ref[at, :])
        return 0

    lax.fori_loop(0, weight_ref.shape[0] // depth, step, 0)
    out_ref[...] = total_ref[...].astype(BF16)


def lower_kernel(count, mixed_ref, upper_ref, projected_ref, *refs):
    parts, out_ref, turned_ref = refs[:NY], refs[-2], refs[-1]
    projected = [projected_ref.at[k] for k in range(NY)]
    pipe_index = lax.axis_index("pipe")
    x_index = lax.axis_index("tensor")
    chunk = turned_ref.shape[0] // NX
    for j in range(NX):
        place = pl.multiple_of(((x_index - j + NX) % NX) * chunk, chunk)
        turned_ref[pl.ds(place, chunk), :] = mixed_ref[j * chunk : (j + 1) * chunk]
    columns = attention_back(
        lambda h: summed(parts, h),
        lambda h: turned_ref[:, h * HD : (h + 1) * HD],
    )
    for h, column in enumerate(columns):
        at = slice(h * HD, (h + 1) * HD)
        lower = column.astype(BF16).astype(F32)
        product = summed(projected, h).astype(F32)
        lower = jnp.sum(lower * product, axis=0, keepdims=True)
        out_ref[:, at] = jnp.where(pipe_index == 1, upper_ref[:, at], lower) * (1.0 / count)


def send_y(value, steps, pipes=(0, 1)):
    pairs = [(NY * p + i, NY * p + (i + steps) % NY) for p in pipes for i in range(NY)]
    return lax.ppermute(value, ("pipe", "y"), pairs)


def send_down(value, steps):
    return lax.ppermute(value, ("pipe", "tensor"), [(NX + i, (i + steps) % NX) for i in range(NX)])


def local(section_input, norm_gain, cotangent, qkv_base, qkv_sign, qkv_scale, out_base):
    inputs = section_input[0]
    tokens, width = inputs.shape
    chunk = tokens // NX
    weight_out = out_base[0]
    sign = qkv_sign[0]
    rows = sign.shape[0]
    weight = (qkv_base[0].astype(F32) + qkv_scale[0][:, None] * sign.astype(F32)).astype(BF16)
    weight_slab = lax.all_gather(weight, "z", axis=0, tiled=False)

    slab = jax.ShapeDtypeStruct((tokens, NZ * HD), BF16)
    quarter_rows = jax.ShapeDtypeStruct((chunk, width), BF16)
    *hidden, own_inputs = call(norm_kernel, (slab,) * NY + (quarter_rows,), (inputs, norm_gain), 10**7, scratch=[pltpu.VMEM((NY, *slab.shape), BF16)])
    hidden_slab = [hidden[0]] + [send_y(hidden[k], k) for k in range(1, NY)]
    later_sign = lax.optimization_barrier((sign, weight_slab, *hidden_slab))[0]
    sign_slab = lax.all_gather(later_sign, "z", axis=0, tiled=False)
    mixed_rows = jax.ShapeDtypeStruct((tokens, QH * HD), BF16)
    mixed_total = [pltpu.VMEM(mixed_rows.shape, F32)]
    grad_mixed, own_cotangent = call(mixed_kernel, (mixed_rows, quarter_rows), (cotangent, weight_out), 10**9, scratch=mixed_total)
    flops = 2 * tokens * rows * width
    packed_rows = jax.ShapeDtypeStruct((tokens, rows), BF16)
    partial = call(packed_kernel, (packed_rows,) * NY, (*hidden_slab, weight_slab), flops)
    parts = [partial[0]] + [send_y(partial[k], -k) for k in (1, 3, 2)]
    is_last = lax.axis_index("pipe") == 1

    grad_upper = call(upper_kernel, packed_rows, (grad_mixed, *parts), 10**8)

    def last_layer():
        near, back_near, far = (send_y(grad_upper, k) for k in (1, 3, 2))
        slab_rows = [grad_upper, near, far, back_near]
        back = call(
            back_kernel,
            jax.ShapeDtypeStruct((NX * NY, chunk, NZ * HD), BF16),
            (*slab_rows, weight_slab),
            flops,
        )
        terms = lax.all_to_all(back, ("tensor", "y"), 0, 0)
        backward = call(
            norm_back_kernel, quarter_rows, (own_inputs, norm_gain, own_cotangent, terms), 10**6
        )
        return (backward, *slab_rows)

    def no_last_layer():
        return (jnp.zeros(quarter_rows.shape, BF16),) + (jnp.zeros(packed_rows.shape, BF16),) * NY

    backward, *slab_rows = lax.cond(is_last, last_layer, no_last_layer)
    arrived = [send_down(backward, j) for j in range(NX)]
    by_y = jax.ShapeDtypeStruct((NY, tokens, rows), BF16)
    signed, upper_total = call(
        sign_kernel,
        (by_y, jax.ShapeDtypeStruct((1, rows), F32)),
        (*hidden_slab, sign_slab, *slab_rows, backward),
        flops,
        unread=1,
    )
    projected = lax.cond(
        is_last,
        lambda: jnp.zeros(by_y.shape, BF16),
        lambda: lax.all_to_all(signed, "y", 0, 0),
    )
    arrived = lax.optimization_barrier((*arrived, projected))[:NX]
    grad_mixed_lower = dot_nn(jnp.concatenate(arrived, axis=0), weight_out).astype(BF16)
    partial_sum = call(
        functools.partial(lower_kernel, tokens * NZ * NY),
        jax.ShapeDtypeStruct((1, rows), F32),
        (grad_mixed_lower, upper_total, projected, *parts),
        10**8,
        scratch=[pltpu.VMEM(mixed_rows.shape, BF16)],
    )
    copies = jnp.broadcast_to(partial_sum, (NZ * NY, rows))
    return jnp.sum(lax.all_to_all(copies, ("z", "y"), 0, 0), axis=0, keepdims=True)


def solution(mesh):
    sizes = mesh.devices.shape
    fine = Mesh(mesh.devices.reshape(sizes[0], sizes[1], NZ, NY), ("pipe", "tensor", "z", "y"))
    dp = ("z", "y")
    placed = (
        P("pipe", dp, None),
        P("pipe", None),
        P(dp, None),
        P("pipe", "tensor", dp),
        P("pipe", "tensor", dp),
        P("pipe", "tensor"),
        P("pipe", None, "tensor"),
    )
    return jax.shard_map(
        local, mesh=fine, in_specs=placed, out_specs=P("pipe", "tensor"), check_vma=False
    )
```

```python
import functools
import math

import jax
import jax.numpy as jnp
from jax import lax
from jax.experimental import pallas as pl
from jax.experimental.pallas import tpu as pltpu
from jax.sharding import Mesh
from jax.sharding import PartitionSpec as P

HD = 128
QH = 8
NY = 4
NX = 4
NZ = 8

F32 = jnp.float32
BF16 = jnp.bfloat16
VMEM = pl.BlockSpec(memory_space=pltpu.VMEM)
ANY = pl.BlockSpec(memory_space=pl.ANY)


def dot_nn(a, b):
    return lax.dot_general(a, b, (((1,), (0,)), ((), ())), preferred_element_type=F32)


def dot_nt(a, b):
    return lax.dot_general(a, b, (((1,), (1,)), ((), ())), preferred_element_type=F32)


def dot_tn(a, b):
    return lax.dot_general(a, b, (((0,), (0,)), ((), ())), preferred_element_type=F32)


def call(kernel, outs, args, flops, vmem=14, unread=0, scratch=()):
    return pl.pallas_call(
        kernel,
        out_shape=outs,
        in_specs=[VMEM] * (len(args) - unread) + [ANY] * unread,
        out_specs=jax.tree.map(lambda _: VMEM, outs),
        scratch_shapes=scratch,
        compiler_params=pltpu.CompilerParams(vmem_limit_bytes=vmem * 1024 * 1024),
        cost_estimate=pl.CostEstimate(flops=flops, bytes_accessed=100000, transcendentals=0),
    )(*args)


def norm_kernel(inputs_ref, gain_ref, *refs):
    quarter_ref, turned_ref = refs[-2:]
    quarter_ref[...] = quarter(inputs_ref)
    y_index = lax.axis_index("y")
    values = inputs_ref[...].astype(F32)
    factor = lax.rsqrt(jnp.mean(values * values, axis=-1, keepdims=True) + 1e-05)
    hidden = (values * factor * gain_ref[...]).astype(BF16)
    for y in range(NY):
        for z in range(NZ):
            block = hidden[:, (z * NY + y) * HD : (z * NY + y + 1) * HD]
            turned_ref[(y - y_index + NY) % NY, :, z * HD : (z + 1) * HD] = block
    for k in range(NY):
        refs[k][...] = turned_ref[k]


def attention_back(packed_of, grads_of):
    factor = 1.0 / math.sqrt(HD)
    queries = jnp.concatenate([packed_of(h) for h in range(QH)], axis=0)
    grads = jnp.concatenate([grads_of(h) for h in range(QH)], axis=0)
    keys, values = packed_of(QH), packed_of(QH + 1)
    length = keys.shape[0]
    scores = dot_nt(queries, keys) * factor
    rows = lax.broadcasted_iota(jnp.int32, scores.shape, 0) % length
    cols = lax.broadcasted_iota(jnp.int32, scores.shape, 1)
    scores = jnp.where(cols <= rows, scores, -1000000000.0)
    top = jnp.max(scores, axis=-1, keepdims=True)
    raised = jnp.exp(scores - top)
    weights = raised / jnp.sum(raised, axis=-1, keepdims=True)
    grad_weights = dot_nt(grads, values)
    inner = jnp.sum(grad_weights * weights, axis=-1, keepdims=True)
    grad_scores = (weights * (grad_weights - inner) * factor).astype(BF16)
    grad_queries = dot_nn(grad_scores, keys)
    heads = [grad_queries[h * length : (h + 1) * length] for h in range(QH)]
    return heads + [dot_tn(grad_scores, queries), dot_tn(weights.astype(BF16), grads)]


def slab_products(hidden, slab_ref):
    for k in range(NY):
        total = None
        for z in range(0, NZ, 2):
            pair = jnp.concatenate([slab_ref[z], slab_ref[z + 1]], axis=1)
            term = dot_nt(hidden[k][:, z * HD : (z + 2) * HD], pair)
            total = term if total is None else total + term
        yield k, total.astype(BF16)


def packed_kernel(*refs):
    for k, product in slab_products(refs[:NY], refs[NY]):
        refs[NY + 1 + k][...] = product


def sign_kernel(*refs):
    hidden, slab_ref, rows = refs[:NY], refs[NY], refs[NY + 1 : 2 * NY + 1]
    out_ref, upper_ref = refs[-2:]
    y_index = lax.axis_index("y")
    upper = None
    for k, product in slab_products(hidden, slab_ref):
        out_ref[(y_index - k + NY) % NY] = product
        term = jnp.sum(rows[k][...].astype(F32) * product.astype(F32), axis=0, keepdims=True)
        upper = term if upper is None else upper + term
    upper_ref[...] = upper


def summed(parts, h):
    at = slice(h * HD, (h + 1) * HD)
    total = parts[0][:, at].astype(F32)
    for part in parts[1:]:
        total = total + part[:, at].astype(F32)
    return total.astype(BF16)


def upper_kernel(grad_ref, *refs):
    parts, grad_packed_ref = refs[:-1], refs[-1]
    columns = attention_back(
        lambda h: summed(parts, h),
        lambda h: grad_ref[:, h * HD : (h + 1) * HD],
    )
    for h, column in enumerate(columns):
        grad_packed_ref[:, h * HD : (h + 1) * HD] = column.astype(BF16)


def back_kernel(*refs):
    rows, slab_ref, out_ref = refs[:NY], refs[NY], refs[-1]
    y_index = lax.axis_index("y")
    chunk = out_ref.shape[1]
    for k in range(NY):
        for z in range(0, NZ, 2):
            pair = jnp.concatenate([slab_ref[z], slab_ref[z + 1]], axis=1)
            term = dot_nn(rows[k][...], pair).astype(BF16)
            for c in range(NX):
                place = c * NY + (y_index - k + NY) % NY
                out_ref[place, :, z * HD : (z + 2) * HD] = term[c * chunk : (c + 1) * chunk]


def norm_back_kernel(inputs_ref, gain_ref, cotangent_ref, terms_ref, out_ref):
    width = out_ref.shape[1]
    values = inputs_ref[...].astype(F32)
    factor = lax.rsqrt(jnp.mean(values * values, axis=-1, keepdims=True) + 1e-05)
    normed = values * factor
    blocks = []
    for z in range(NZ):
        for y in range(NY):
            at = slice(z * HD, (z + 1) * HD)
            block = terms_ref[y, :, at].astype(F32)
            for x in range(1, NX):
                block = block + terms_ref[x * NY + y, :, at].astype(F32)
            blocks.append(block)
    grad = jnp.concatenate(blocks, axis=1) * gain_ref[...]
    mean = jnp.sum(grad * normed, axis=-1, keepdims=True) * (1.0 / width)
    out_ref[...] = (cotangent_ref[...].astype(F32) + factor * (grad - normed * mean)).astype(BF16)


def quarter(ref):
    chunk = ref.shape[0] // NX
    return ref[pl.ds(pl.multiple_of(lax.axis_index("tensor") * chunk, chunk), chunk), :]


def mixed_kernel(rows_ref, weight_ref, out_ref, quarter_ref, total_ref):
    depth = 512
    quarter_ref[...] = quarter(rows_ref)
    total_ref[...] = jnp.zeros_like(total_ref)

    def step(i, _):
        at = pl.ds(pl.multiple_of(i * depth, depth), depth)
        total_ref[...] += dot_nn(rows_ref[:, at], weight_ref[at, :])
        return 0

    lax.fori_loop(0, weight_ref.shape[0] // depth, step, 0)
    out_ref[...] = total_ref[...].astype(BF16)


def lower_kernel(count, mixed_ref, upper_ref, projected_ref, *refs):
    parts, out_ref, turned_ref = refs[:NY], refs[-2], refs[-1]
    projected = [projected_ref.at[k] for k in range(NY)]
    pipe_index = lax.axis_index("pipe")
    x_index = lax.axis_index("tensor")
    chunk = turned_ref.shape[0] // NX
    for j in range(NX):
        place = pl.multiple_of(((x_index - j + NX) % NX) * chunk, chunk)
        turned_ref[pl.ds(place, chunk), :] = mixed_ref[j * chunk : (j + 1) * chunk]
    columns = attention_back(
        lambda h: summed(parts, h),
        lambda h: turned_ref[:, h * HD : (h + 1) * HD],
    )
    for h, column in enumerate(columns):
        at = slice(h * HD, (h + 1) * HD)
        lower = column.astype(BF16).astype(F32)
        product = summed(projected, h).astype(F32)
        lower = jnp.sum(lower * product, axis=0, keepdims=True)
        out_ref[:, at] = jnp.where(pipe_index == 1, upper_ref[:, at], lower) * (1.0 / count)


def send_y(value, steps, pipes=(0, 1)):
    pairs = [(NY * p + i, NY * p + (i + steps) % NY) for p in pipes for i in range(NY)]
    return lax.ppermute(value, ("pipe", "y"), pairs)


def send_down(value, steps):
    return lax.ppermute(value, ("pipe", "tensor"), [(NX + i, (i + steps) % NX) for i in range(NX)])


def local(section_input, norm_gain, cotangent, qkv_base, qkv_sign, qkv_scale, out_base):
    inputs = section_input[0]
    tokens, width = inputs.shape
    chunk = tokens // NX
    weight_out = out_base[0]
    sign = qkv_sign[0]
    rows = sign.shape[0]
    weight = (qkv_base[0].astype(F32) + qkv_scale[0][:, None] * sign.astype(F32)).astype(BF16)
    weight_slab = lax.all_gather(weight, "z", axis=0, tiled=False)

    slab = jax.ShapeDtypeStruct((tokens, NZ * HD), BF16)
    quarter_rows = jax.ShapeDtypeStruct((chunk, width), BF16)
    *hidden, own_inputs = call(norm_kernel, (slab,) * NY + (quarter_rows,), (inputs, norm_gain), 10**7, scratch=[pltpu.VMEM((NY, *slab.shape), BF16)])
    hidden_slab = [hidden[0]] + [send_y(hidden[k], k) for k in range(1, NY)]
    later_sign = lax.optimization_barrier((sign, weight_slab, *hidden_slab))[0]
    sign_slab = lax.all_gather(later_sign, "z", axis=0, tiled=False)
    mixed_rows = jax.ShapeDtypeStruct((tokens, QH * HD), BF16)
    mixed_total = [pltpu.VMEM(mixed_rows.shape, F32)]
    grad_mixed, own_cotangent = call(mixed_kernel, (mixed_rows, quarter_rows), (cotangent, weight_out), 10**9, scratch=mixed_total)
    flops = 2 * tokens * rows * width
    packed_rows = jax.ShapeDtypeStruct((tokens, rows), BF16)
    partial = call(packed_kernel, (packed_rows,) * NY, (*hidden_slab, weight_slab), flops)
    parts = [partial[0]] + [send_y(partial[k], -k) for k in (1, 3, 2)]
    is_last = lax.axis_index("pipe") == 1

    grad_upper = call(upper_kernel, packed_rows, (grad_mixed, *parts), 10**8)

    def last_layer():
        near, back_near, far = (send_y(grad_upper, k) for k in (1, 3, 2))
        slab_rows = [grad_upper, near, far, back_near]
        back = call(
            back_kernel,
            jax.ShapeDtypeStruct((NX * NY, chunk, NZ * HD), BF16),
            (*slab_rows, weight_slab),
            flops,
        )
        terms = lax.all_to_all(back, ("tensor", "y"), 0, 0)
        backward = call(
            norm_back_kernel, quarter_rows, (own_inputs, norm_gain, own_cotangent, terms), 10**6
        )
        return (backward, *slab_rows)

    def no_last_layer():
        return (jnp.zeros(quarter_rows.shape, BF16),) + (jnp.zeros(packed_rows.shape, BF16),) * NY

    backward, *slab_rows = lax.cond(is_last, last_layer, no_last_layer)
    arrived = [send_down(backward, j) for j in range(NX)]
    by_y = jax.ShapeDtypeStruct((NY, tokens, rows), BF16)
    signed, upper_total = call(
        sign_kernel,
        (by_y, jax.ShapeDtypeStruct((1, rows), F32)),
        (*hidden_slab, sign_slab, *slab_rows, backward),
        flops,
        unread=1,
    )
    projected = lax.cond(
        is_last,
        lambda: jnp.zeros(by_y.shape, BF16),
        lambda: lax.all_to_all(signed, "y", 0, 0),
    )
    arrived = lax.optimization_barrier((*arrived, projected))[:NX]
    grad_mixed_lower = lax.cond(
        is_last,
        lambda: jnp.zeros(mixed_rows.shape, BF16),
        lambda: dot_nn(jnp.concatenate(arrived, axis=0), weight_out).astype(BF16),
    )
    partial_sum = call(
        functools.partial(lower_kernel, tokens * NZ * NY),
        jax.ShapeDtypeStruct((1, rows), F32),
        (grad_mixed_lower, upper_total, projected, *parts),
        10**8,
        scratch=[pltpu.VMEM(mixed_rows.shape, BF16)],
    )
    copies = jnp.broadcast_to(partial_sum, (NZ * NY, rows))
    return jnp.sum(lax.all_to_all(copies, ("z", "y"), 0, 0), axis=0, keepdims=True)


def solution(mesh):
    sizes = mesh.devices.shape
    fine = Mesh(mesh.devices.reshape(sizes[0], sizes[1], NZ, NY), ("pipe", "tensor", "z", "y"))
    dp = ("z", "y")
    placed = (
        P("pipe", dp, None),
        P("pipe", None),
        P(dp, None),
        P("pipe", "tensor", dp),
        P("pipe", "tensor", dp),
        P("pipe", "tensor"),
        P("pipe", None, "tensor"),
    )
    return jax.shard_map(
        local, mesh=fine, in_specs=placed, out_specs=P("pipe", "tensor"), check_vma=False
    )
```

```python
import functools
import math

import jax
import jax.numpy as jnp
from jax import lax
from jax.experimental import pallas as pl
from jax.experimental.pallas import tpu as pltpu
from jax.sharding import Mesh
from jax.sharding import PartitionSpec as P

HD = 128
QH = 8
NY = 4
NX = 4
NZ = 8

F32 = jnp.float32
BF16 = jnp.bfloat16
VMEM = pl.BlockSpec(memory_space=pltpu.VMEM)
ANY = pl.BlockSpec(memory_space=pl.ANY)


def dot_nn(a, b):
    return lax.dot_general(a, b, (((1,), (0,)), ((), ())), preferred_element_type=F32)


def dot_nt(a, b):
    return lax.dot_general(a, b, (((1,), (1,)), ((), ())), preferred_element_type=F32)


def dot_tn(a, b):
    return lax.dot_general(a, b, (((0,), (0,)), ((), ())), preferred_element_type=F32)


def call(kernel, outs, args, flops, vmem=14, unread=0, scratch=()):
    return pl.pallas_call(
        kernel,
        out_shape=outs,
        in_specs=[VMEM] * (len(args) - unread) + [ANY] * unread,
        out_specs=jax.tree.map(lambda _: VMEM, outs),
        scratch_shapes=scratch,
        compiler_params=pltpu.CompilerParams(vmem_limit_bytes=vmem * 1024 * 1024),
        cost_estimate=pl.CostEstimate(flops=flops, bytes_accessed=100000, transcendentals=0),
    )(*args)


def norm_kernel(inputs_ref, gain_ref, *refs):
    quarter_ref, turned_ref = refs[-2:]
    quarter_ref[...] = quarter(inputs_ref)
    y_index = lax.axis_index("y")
    values = inputs_ref[...].astype(F32)
    factor = lax.rsqrt(jnp.mean(values * values, axis=-1, keepdims=True) + 1e-05)
    hidden = (values * factor * gain_ref[...]).astype(BF16)
    for y in range(NY):
        for z in range(NZ):
            block = hidden[:, (z * NY + y) * HD : (z * NY + y + 1) * HD]
            turned_ref[(y - y_index + NY) % NY, :, z * HD : (z + 1) * HD] = block
    for k in range(NY):
        refs[k][...] = turned_ref[k]


def attention_back(packed_of, grads_of):
    factor = 1.0 / math.sqrt(HD)
    queries = jnp.concatenate([packed_of(h) for h in range(QH)], axis=0)
    grads = jnp.concatenate([grads_of(h) for h in range(QH)], axis=0)
    keys, values = packed_of(QH), packed_of(QH + 1)
    length = keys.shape[0]
    scores = dot_nt(queries, keys) * factor
    rows = lax.broadcasted_iota(jnp.int32, scores.shape, 0) % length
    cols = lax.broadcasted_iota(jnp.int32, scores.shape, 1)
    scores = jnp.where(cols <= rows, scores, -1000000000.0)
    top = jnp.max(scores, axis=-1, keepdims=True)
    raised = jnp.exp(scores - top)
    weights = raised / jnp.sum(raised, axis=-1, keepdims=True)
    grad_weights = dot_nt(grads, values)
    inner = jnp.sum(grad_weights * weights, axis=-1, keepdims=True)
    grad_scores = (weights * (grad_weights - inner) * factor).astype(BF16)
    grad_queries = dot_nn(grad_scores, keys)
    heads = [grad_queries[h * length : (h + 1) * length] for h in range(QH)]
    return heads + [dot_tn(grad_scores, queries), dot_tn(weights.astype(BF16), grads)]


def slab_products(hidden, slab_ref):
    rows = jnp.concatenate([ref[...] for ref in hidden], axis=0)
    step = 2 * HD
    for c in range(0, slab_ref.shape[1], step):
        part = jnp.concatenate([slab_ref[z, c : c + step, :] for z in range(NZ)], axis=1)
        yield slice(c, c + step), dot_nt(rows, part).astype(BF16)


def packed_kernel(*refs):
    length = refs[0].shape[0]
    for at, product in slab_products(refs[:NY], refs[NY]):
        for k in range(NY):
            refs[NY + 1 + k][:, at] = product[k * length : (k + 1) * length]


def sign_kernel(*refs):
    hidden, slab_ref, rows = refs[:NY], refs[NY], refs[NY + 1 : 2 * NY + 1]
    out_ref, upper_ref, held_ref, sems = refs[-4:]
    y_index = lax.axis_index("y")
    length = refs[0].shape[0]
    for at, product in slab_products(hidden, slab_ref):
        for k in range(NY):
            out_ref[(y_index - k + NY) % NY, :, at] = product[k * length : (k + 1) * length]
    upper_ref[...] = jnp.zeros_like(upper_ref)

    @pl.when(lax.axis_index("pipe") == 1)
    def _():
        copies = [pltpu.make_async_copy(rows[k], held_ref.at[k], sems.at[k]) for k in range(NY)]
        for copy in copies:
            copy.start()
        for k in range(NY):
            copies[k].wait()
            product = out_ref[(y_index - k + NY) % NY].astype(F32)
            upper_ref[...] += jnp.sum(held_ref[k].astype(F32) * product, axis=0, keepdims=True)


def summed(parts, h):
    at = slice(h * HD, (h + 1) * HD)
    total = parts[0][:, at].astype(F32)
    for part in parts[1:]:
        total = total + part[:, at].astype(F32)
    return total.astype(BF16)


def upper_kernel(grad_ref, *refs):
    parts, grad_packed_ref = refs[:-1], refs[-1]
    columns = attention_back(
        lambda h: summed(parts, h),
        lambda h: grad_ref[:, h * HD : (h + 1) * HD],
    )
    for h, column in enumerate(columns):
        grad_packed_ref[:, h * HD : (h + 1) * HD] = column.astype(BF16)


def back_kernel(*refs):
    rows, slab_ref, out_ref = refs[:NY], refs[NY], refs[-1]
    y_index = lax.axis_index("y")
    chunk = out_ref.shape[1]
    length = rows[0].shape[0]
    grads = jnp.concatenate([ref[...] for ref in rows], axis=0)
    for z in range(0, NZ, 2):
        pair = jnp.concatenate([slab_ref[z], slab_ref[z + 1]], axis=1)
        terms = dot_nn(grads, pair).astype(BF16)
        for k in range(NY):
            for c in range(NX):
                place = c * NY + (y_index - k + NY) % NY
                start = k * length + c * chunk
                out_ref[place, :, z * HD : (z + 2) * HD] = terms[start : start + chunk]


def norm_back_kernel(inputs_ref, gain_ref, cotangent_ref, terms_ref, out_ref):
    width = out_ref.shape[1]
    values = inputs_ref[...].astype(F32)
    factor = lax.rsqrt(jnp.mean(values * values, axis=-1, keepdims=True) + 1e-05)
    normed = values * factor
    blocks = []
    for z in range(NZ):
        for y in range(NY):
            at = slice(z * HD, (z + 1) * HD)
            block = terms_ref[y, :, at].astype(F32)
            for x in range(1, NX):
                block = block + terms_ref[x * NY + y, :, at].astype(F32)
            blocks.append(block)
    grad = jnp.concatenate(blocks, axis=1) * gain_ref[...]
    mean = jnp.sum(grad * normed, axis=-1, keepdims=True) * (1.0 / width)
    out_ref[...] = (cotangent_ref[...].astype(F32) + factor * (grad - normed * mean)).astype(BF16)


def quarter(ref):
    chunk = ref.shape[0] // NX
    return ref[pl.ds(pl.multiple_of(lax.axis_index("tensor") * chunk, chunk), chunk), :]


def mixed_kernel(rows_ref, weight_ref, out_ref, quarter_ref, total_ref):
    depth = 512
    quarter_ref[...] = quarter(rows_ref)
    total_ref[...] = jnp.zeros_like(total_ref)

    def step(i, _):
        at = pl.ds(pl.multiple_of(i * depth, depth), depth)
        total_ref[...] += dot_nn(rows_ref[:, at], weight_ref[at, :])
        return 0

    lax.fori_loop(0, weight_ref.shape[0] // depth, step, 0)
    out_ref[...] = total_ref[...].astype(BF16)


def lower_kernel(count, mixed_ref, upper_ref, *refs):
    parts, projected_ref, out_ref, turned_ref, held_ref, sem = refs[:NY], *refs[NY:]
    copy = pltpu.make_async_copy(projected_ref, held_ref, sem)
    copy.start()
    projected = [held_ref.at[k] for k in range(NY)]
    pipe_index = lax.axis_index("pipe")
    x_index = lax.axis_index("tensor")
    chunk = turned_ref.shape[0] // NX
    for j in range(NX):
        place = pl.multiple_of(((x_index - j + NX) % NX) * chunk, chunk)
        turned_ref[pl.ds(place, chunk), :] = mixed_ref[j * chunk : (j + 1) * chunk]
    columns = attention_back(
        lambda h: summed(parts, h),
        lambda h: turned_ref[:, h * HD : (h + 1) * HD],
    )
    copy.wait()
    for h, column in enumerate(columns):
        at = slice(h * HD, (h + 1) * HD)
        lower = column.astype(BF16).astype(F32)
        product = summed(projected, h).astype(F32)
        lower = jnp.sum(lower * product, axis=0, keepdims=True)
        out_ref[:, at] = jnp.where(pipe_index == 1, upper_ref[:, at], lower) * (1.0 / count)


def send_y(value, steps, pipes=(0, 1)):
    pairs = [(NY * p + i, NY * p + (i + steps) % NY) for p in pipes for i in range(NY)]
    return lax.ppermute(value, ("pipe", "y"), pairs)


def send_down(value, steps):
    return lax.ppermute(value, ("pipe", "tensor"), [(NX + i, (i + steps) % NX) for i in range(NX)])


def local(section_input, norm_gain, cotangent, qkv_base, qkv_sign, qkv_scale, out_base):
    inputs = section_input[0]
    tokens, width = inputs.shape
    chunk = tokens // NX
    weight_out = out_base[0]
    sign = qkv_sign[0]
    rows = sign.shape[0]
    weight = (qkv_base[0].astype(F32) + qkv_scale[0][:, None] * sign.astype(F32)).astype(BF16)
    weight_slab = lax.all_gather(weight, "z", axis=0, tiled=False)

    slab = jax.ShapeDtypeStruct((tokens, NZ * HD), BF16)
    quarter_rows = jax.ShapeDtypeStruct((chunk, width), BF16)
    *hidden, own_inputs = call(norm_kernel, (slab,) * NY + (quarter_rows,), (inputs, norm_gain), 10**7, scratch=[pltpu.VMEM((NY, *slab.shape), BF16)])
    hidden_slab = [hidden[0]] + [send_y(hidden[k], k) for k in range(1, NY)]
    later_sign = lax.optimization_barrier((sign, weight_slab, *hidden_slab))[0]
    sign_slab = lax.all_gather(later_sign, "z", axis=0, tiled=False)
    mixed_rows = jax.ShapeDtypeStruct((tokens, QH * HD), BF16)
    mixed_total = [pltpu.VMEM(mixed_rows.shape, F32)]
    grad_mixed, own_cotangent = call(mixed_kernel, (mixed_rows, quarter_rows), (cotangent, weight_out), 10**9, scratch=mixed_total)
    flops = 2 * tokens * rows * width
    packed_rows = jax.ShapeDtypeStruct((tokens, rows), BF16)
    partial = call(packed_kernel, (packed_rows,) * NY, (*hidden_slab, weight_slab), flops)
    parts = [partial[0]] + [send_y(partial[k], -k) for k in (1, 3, 2)]
    is_last = lax.axis_index("pipe") == 1

    grad_upper = call(upper_kernel, packed_rows, (grad_mixed, *parts), 10**8)

    def last_layer():
        near, back_near, far = (send_y(grad_upper, k) for k in (1, 3, 2))
        slab_rows = [grad_upper, near, far, back_near]
        back = call(
            back_kernel,
            jax.ShapeDtypeStruct((NX * NY, chunk, NZ * HD), BF16),
            (*slab_rows, weight_slab),
            flops,
        )
        terms = lax.all_to_all(back, ("tensor", "y"), 0, 0)
        backward = call(
            norm_back_kernel, quarter_rows, (own_inputs, norm_gain, own_cotangent, terms), 10**6
        )
        return (backward, *slab_rows)

    def no_last_layer():
        return (jnp.zeros(quarter_rows.shape, BF16),) + (jnp.zeros(packed_rows.shape, BF16),) * NY

    backward, *slab_rows = lax.cond(is_last, last_layer, no_last_layer)
    arrived = [send_down(backward, j) for j in range(NX)]
    by_y = jax.ShapeDtypeStruct((NY, tokens, rows), BF16)
    signed, upper_total = call(
        sign_kernel,
        (by_y, jax.ShapeDtypeStruct((1, rows), F32)),
        (*hidden_slab, sign_slab, *slab_rows, backward),
        flops,
        unread=NY + 1,
        scratch=[pltpu.VMEM(by_y.shape, BF16), pltpu.SemaphoreType.DMA((NY,))],
    )
    projected = lax.cond(
        is_last,
        lambda: jnp.zeros(by_y.shape, BF16),
        lambda: lax.all_to_all(signed, "y", 0, 0),
    )
    arrived = lax.optimization_barrier((*arrived, projected))[:NX]
    grad_mixed_lower = lax.cond(
        is_last,
        lambda: jnp.zeros(mixed_rows.shape, BF16),
        lambda: dot_nn(jnp.concatenate(arrived, axis=0), weight_out).astype(BF16),
    )
    partial_sum = call(
        functools.partial(lower_kernel, tokens * NZ * NY),
        jax.ShapeDtypeStruct((1, rows), F32),
        (grad_mixed_lower, upper_total, *parts, projected),
        10**8,
        unread=1,
        scratch=[
            pltpu.VMEM(mixed_rows.shape, BF16),
            pltpu.VMEM(by_y.shape, BF16),
            pltpu.SemaphoreType.DMA,
        ],
    )
    copies = jnp.broadcast_to(partial_sum, (NZ * NY, rows))
    return jnp.sum(lax.all_to_all(copies, ("z", "y"), 0, 0), axis=0, keepdims=True)


def solution(mesh):
    sizes = mesh.devices.shape
    fine = Mesh(mesh.devices.reshape(sizes[0], sizes[1], NZ, NY), ("pipe", "tensor", "z", "y"))
    dp = ("z", "y")
    placed = (
        P("pipe", dp, None),
        P("pipe", None),
        P(dp, None),
        P("pipe", "tensor", dp),
        P("pipe", "tensor", dp),
        P("pipe", "tensor"),
        P("pipe", None, "tensor"),
    )
    return jax.shard_map(
        local, mesh=fine, in_specs=placed, out_specs=P("pipe", "tensor"), check_vma=False
    )
```

```python
import functools
import math

import jax
import jax.numpy as jnp
from jax import lax
from jax.experimental import pallas as pl
from jax.experimental.pallas import tpu as pltpu
from jax.sharding import Mesh
from jax.sharding import PartitionSpec as P

HD = 128
QH = 8
NY = 4
NX = 4
NZ = 8

F32 = jnp.float32
BF16 = jnp.bfloat16
VMEM = pl.BlockSpec(memory_space=pltpu.VMEM)
ANY = pl.BlockSpec(memory_space=pl.ANY)


def dot_nn(a, b):
    return lax.dot_general(a, b, (((1,), (0,)), ((), ())), preferred_element_type=F32)


def dot_nt(a, b):
    return lax.dot_general(a, b, (((1,), (1,)), ((), ())), preferred_element_type=F32)


def dot_tn(a, b):
    return lax.dot_general(a, b, (((0,), (0,)), ((), ())), preferred_element_type=F32)


def call(kernel, outs, args, flops, vmem=14, unread=0, scratch=()):
    return pl.pallas_call(
        kernel,
        out_shape=outs,
        in_specs=[VMEM] * (len(args) - unread) + [ANY] * unread,
        out_specs=jax.tree.map(lambda _: VMEM, outs),
        scratch_shapes=scratch,
        compiler_params=pltpu.CompilerParams(vmem_limit_bytes=vmem * 1024 * 1024),
        cost_estimate=pl.CostEstimate(flops=flops, bytes_accessed=100000, transcendentals=0),
    )(*args)


def norm_kernel(inputs_ref, gain_ref, *refs):
    quarter_ref, turned_ref = refs[-2:]
    quarter_ref[...] = quarter(inputs_ref)
    y_index = lax.axis_index("y")
    values = inputs_ref[...].astype(F32)
    factor = lax.rsqrt(jnp.mean(values * values, axis=-1, keepdims=True) + 1e-05)
    hidden = (values * factor * gain_ref[...]).astype(BF16)
    for y in range(NY):
        for z in range(NZ):
            block = hidden[:, (z * NY + y) * HD : (z * NY + y + 1) * HD]
            turned_ref[(y - y_index + NY) % NY, :, z * HD : (z + 1) * HD] = block
    for k in range(NY):
        refs[k][...] = turned_ref[k]


def attention_weights(packed_of):
    queries = jnp.concatenate([packed_of(h) for h in range(QH)], axis=0)
    keys = packed_of(QH)
    scores = dot_nt(queries, keys) * (1.0 / math.sqrt(HD))
    rows = lax.broadcasted_iota(jnp.int32, scores.shape, 0) % keys.shape[0]
    cols = lax.broadcasted_iota(jnp.int32, scores.shape, 1)
    scores = jnp.where(cols <= rows, scores, -1000000000.0)
    top = jnp.max(scores, axis=-1, keepdims=True)
    raised = jnp.exp(scores - top)
    return raised / jnp.sum(raised, axis=-1, keepdims=True)


def attention_back(packed_of, grads_of, weights):
    factor = 1.0 / math.sqrt(HD)
    queries = jnp.concatenate([packed_of(h) for h in range(QH)], axis=0)
    grads = jnp.concatenate([grads_of(h) for h in range(QH)], axis=0)
    keys, values = packed_of(QH), packed_of(QH + 1)
    length = keys.shape[0]
    grad_weights = dot_nt(grads, values)
    inner = jnp.sum(grad_weights * weights, axis=-1, keepdims=True)
    grad_scores = (weights * (grad_weights - inner) * factor).astype(BF16)
    grad_queries = dot_nn(grad_scores, keys)
    heads = [grad_queries[h * length : (h + 1) * length] for h in range(QH)]
    return heads + [dot_tn(grad_scores, queries), dot_tn(weights.astype(BF16), grads)]


def slab_products(hidden, slab_ref):
    rows = jnp.concatenate([ref[...] for ref in hidden], axis=0)
    step = 2 * HD
    for c in range(0, slab_ref.shape[1], step):
        part = jnp.concatenate([slab_ref[z, c : c + step, :] for z in range(NZ)], axis=1)
        yield slice(c, c + step), dot_nt(rows, part).astype(BF16)


def packed_kernel(*refs):
    length = refs[0].shape[0]
    for at, product in slab_products(refs[:NY], refs[NY]):
        for k in range(NY):
            refs[NY + 1 + k][:, at] = product[k * length : (k + 1) * length]


def sign_kernel(*refs):
    hidden, slab_ref, rows = refs[:NY], refs[NY], refs[NY + 1 : 2 * NY + 1]
    out_ref, upper_ref, held_ref, sems = refs[-4:]
    y_index = lax.axis_index("y")
    length = refs[0].shape[0]
    for at, product in slab_products(hidden, slab_ref):
        for k in range(NY):
            out_ref[(y_index - k + NY) % NY, :, at] = product[k * length : (k + 1) * length]
    upper_ref[...] = jnp.zeros_like(upper_ref)

    @pl.when(lax.axis_index("pipe") == 1)
    def _():
        copies = [pltpu.make_async_copy(rows[k], held_ref.at[k], sems.at[k]) for k in range(NY)]
        for copy in copies:
            copy.start()
        for k in range(NY):
            copies[k].wait()
            product = out_ref[(y_index - k + NY) % NY].astype(F32)
            upper_ref[...] += jnp.sum(held_ref[k].astype(F32) * product, axis=0, keepdims=True)


def summed(parts, h):
    at = slice(h * HD, (h + 1) * HD)
    total = parts[0][:, at].astype(F32)
    for part in parts[1:]:
        total = total + part[:, at].astype(F32)
    return total.astype(BF16)


def upper_kernel(grad_ref, *refs):
    parts, grad_packed_ref = refs[:-1], refs[-1]
    packed_of = lambda h: summed(parts, h)
    columns = attention_back(
        packed_of, lambda h: grad_ref[:, h * HD : (h + 1) * HD], attention_weights(packed_of)
    )
    for h, column in enumerate(columns):
        grad_packed_ref[:, h * HD : (h + 1) * HD] = column.astype(BF16)


def back_kernel(*refs):
    rows, slab_ref, out_ref = refs[:NY], refs[NY], refs[-1]
    y_index = lax.axis_index("y")
    chunk = out_ref.shape[1]
    length = rows[0].shape[0]
    grads = jnp.concatenate([ref[...] for ref in rows], axis=0)
    for z in range(0, NZ, 2):
        pair = jnp.concatenate([slab_ref[z], slab_ref[z + 1]], axis=1)
        terms = dot_nn(grads, pair).astype(BF16)
        for k in range(NY):
            for c in range(NX):
                place = c * NY + (y_index - k + NY) % NY
                start = k * length + c * chunk
                out_ref[place, :, z * HD : (z + 2) * HD] = terms[start : start + chunk]


def norm_back_kernel(inputs_ref, gain_ref, cotangent_ref, terms_ref, out_ref):
    width = out_ref.shape[1]
    values = inputs_ref[...].astype(F32)
    factor = lax.rsqrt(jnp.mean(values * values, axis=-1, keepdims=True) + 1e-05)
    normed = values * factor
    blocks = []
    for z in range(NZ):
        for y in range(NY):
            at = slice(z * HD, (z + 1) * HD)
            block = terms_ref[y, :, at].astype(F32)
            for x in range(1, NX):
                block = block + terms_ref[x * NY + y, :, at].astype(F32)
            blocks.append(block)
    grad = jnp.concatenate(blocks, axis=1) * gain_ref[...]
    mean = jnp.sum(grad * normed, axis=-1, keepdims=True) * (1.0 / width)
    out_ref[...] = (cotangent_ref[...].astype(F32) + factor * (grad - normed * mean)).astype(BF16)


def quarter(ref):
    chunk = ref.shape[0] // NX
    return ref[pl.ds(pl.multiple_of(lax.axis_index("tensor") * chunk, chunk), chunk), :]


def mixed_kernel(rows_ref, weight_ref, out_ref, quarter_ref, total_ref):
    depth = 512
    quarter_ref[...] = quarter(rows_ref)
    total_ref[...] = jnp.zeros_like(total_ref)

    def step(i, _):
        at = pl.ds(pl.multiple_of(i * depth, depth), depth)
        total_ref[...] += dot_nn(rows_ref[:, at], weight_ref[at, :])
        return 0

    lax.fori_loop(0, weight_ref.shape[0] // depth, step, 0)
    out_ref[...] = total_ref[...].astype(BF16)


def ready_kernel(*refs):
    parts, packed_ref, weights_ref = refs[:NY], refs[NY], refs[NY + 1]
    for h in range(QH + 2):
        packed_ref[:, h * HD : (h + 1) * HD] = summed(parts, h)
    weights_ref[...] = attention_weights(lambda h: packed_ref[:, h * HD : (h + 1) * HD])


def lower_kernel(count, mixed_ref, upper_ref, packed_ref, weights_ref, *refs):
    projected_ref, out_ref, turned_ref, held_ref, sem = refs
    copy = pltpu.make_async_copy(projected_ref, held_ref, sem)
    copy.start()
    projected = [held_ref.at[k] for k in range(NY)]
    pipe_index = lax.axis_index("pipe")
    x_index = lax.axis_index("tensor")
    chunk = turned_ref.shape[0] // NX
    for j in range(NX):
        place = pl.multiple_of(((x_index - j + NX) % NX) * chunk, chunk)
        turned_ref[pl.ds(place, chunk), :] = mixed_ref[j * chunk : (j + 1) * chunk]
    columns = attention_back(
        lambda h: packed_ref[:, h * HD : (h + 1) * HD],
        lambda h: turned_ref[:, h * HD : (h + 1) * HD],
        weights_ref[...],
    )
    copy.wait()
    for h, column in enumerate(columns):
        at = slice(h * HD, (h + 1) * HD)
        lower = column.astype(BF16).astype(F32)
        product = summed(projected, h).astype(F32)
        lower = jnp.sum(lower * product, axis=0, keepdims=True)
        out_ref[:, at] = jnp.where(pipe_index == 1, upper_ref[:, at], lower) * (1.0 / count)


def send_y(value, steps, pipes=(0, 1)):
    pairs = [(NY * p + i, NY * p + (i + steps) % NY) for p in pipes for i in range(NY)]
    return lax.ppermute(value, ("pipe", "y"), pairs)


def send_down(value, steps):
    return lax.ppermute(value, ("pipe", "tensor"), [(NX + i, (i + steps) % NX) for i in range(NX)])


def local(section_input, norm_gain, cotangent, qkv_base, qkv_sign, qkv_scale, out_base):
    inputs = section_input[0]
    tokens, width = inputs.shape
    chunk = tokens // NX
    weight_out = out_base[0]
    sign = qkv_sign[0]
    rows = sign.shape[0]
    weight = (qkv_base[0].astype(F32) + qkv_scale[0][:, None] * sign.astype(F32)).astype(BF16)
    weight_slab = lax.all_gather(weight, "z", axis=0, tiled=False)

    slab = jax.ShapeDtypeStruct((tokens, NZ * HD), BF16)
    quarter_rows = jax.ShapeDtypeStruct((chunk, width), BF16)
    *hidden, own_inputs = call(norm_kernel, (slab,) * NY + (quarter_rows,), (inputs, norm_gain), 10**7, scratch=[pltpu.VMEM((NY, *slab.shape), BF16)])
    hidden_slab = [hidden[0]] + [send_y(hidden[k], k) for k in range(1, NY)]
    later_sign = lax.optimization_barrier((sign, weight_slab, *hidden_slab))[0]
    sign_slab = lax.all_gather(later_sign, "z", axis=0, tiled=False)
    mixed_rows = jax.ShapeDtypeStruct((tokens, QH * HD), BF16)
    mixed_total = [pltpu.VMEM(mixed_rows.shape, F32)]
    grad_mixed, own_cotangent = call(mixed_kernel, (mixed_rows, quarter_rows), (cotangent, weight_out), 10**9, scratch=mixed_total)
    flops = 2 * tokens * rows * width
    packed_rows = jax.ShapeDtypeStruct((tokens, rows), BF16)
    partial = call(packed_kernel, (packed_rows,) * NY, (*hidden_slab, weight_slab), flops)
    parts = [partial[0]] + [send_y(partial[k], -k) for k in (1, 3, 2)]
    is_last = lax.axis_index("pipe") == 1

    grad_upper = call(upper_kernel, packed_rows, (grad_mixed, *parts), 10**8)

    def last_layer():
        near, back_near, far = (send_y(grad_upper, k) for k in (1, 3, 2))
        slab_rows = [grad_upper, near, far, back_near]
        back = call(
            back_kernel,
            jax.ShapeDtypeStruct((NX * NY, chunk, NZ * HD), BF16),
            (*slab_rows, weight_slab),
            flops,
        )
        terms = lax.all_to_all(back, ("tensor", "y"), 0, 0)
        backward = call(
            norm_back_kernel, quarter_rows, (own_inputs, norm_gain, own_cotangent, terms), 10**6
        )
        return (backward, *slab_rows)

    def no_last_layer():
        return (jnp.zeros(quarter_rows.shape, BF16),) + (jnp.zeros(packed_rows.shape, BF16),) * NY

    backward, *slab_rows = lax.cond(is_last, last_layer, no_last_layer)
    arrived = [send_down(backward, j) for j in range(NX)]
    by_y = jax.ShapeDtypeStruct((NY, tokens, rows), BF16)
    signed, upper_total = call(
        sign_kernel,
        (by_y, jax.ShapeDtypeStruct((1, rows), F32)),
        (*hidden_slab, sign_slab, *slab_rows, backward),
        flops,
        unread=NY + 1,
        scratch=[pltpu.VMEM(by_y.shape, BF16), pltpu.SemaphoreType.DMA((NY,))],
    )
    ready_shapes = (packed_rows, jax.ShapeDtypeStruct((QH * tokens, tokens), F32))
    projected, packed, weights = lax.cond(
        is_last,
        lambda: tuple(jnp.zeros(shape.shape, shape.dtype) for shape in (by_y, *ready_shapes)),
        lambda: (lax.all_to_all(signed, "y", 0, 0), *call(ready_kernel, ready_shapes, parts, 10**8)),
    )
    arrived = lax.optimization_barrier((*arrived, projected))[:NX]
    grad_mixed_lower = lax.cond(
        is_last,
        lambda: jnp.zeros(mixed_rows.shape, BF16),
        lambda: dot_nn(jnp.concatenate(arrived, axis=0), weight_out).astype(BF16),
    )
    partial_sum = call(
        functools.partial(lower_kernel, tokens * NZ * NY),
        jax.ShapeDtypeStruct((1, rows), F32),
        (grad_mixed_lower, upper_total, packed, weights, projected),
        10**8,
        unread=1,
        scratch=[
            pltpu.VMEM(mixed_rows.shape, BF16),
            pltpu.VMEM(by_y.shape, BF16),
            pltpu.SemaphoreType.DMA,
        ],
    )
    copies = jnp.broadcast_to(partial_sum, (NZ * NY, rows))
    return jnp.sum(lax.all_to_all(copies, ("z", "y"), 0, 0), axis=0, keepdims=True)


def solution(mesh):
    sizes = mesh.devices.shape
    fine = Mesh(mesh.devices.reshape(sizes[0], sizes[1], NZ, NY), ("pipe", "tensor", "z", "y"))
    dp = ("z", "y")
    placed = (
        P("pipe", dp, None),
        P("pipe", None),
        P(dp, None),
        P("pipe", "tensor", dp),
        P("pipe", "tensor", dp),
        P("pipe", "tensor"),
        P("pipe", None, "tensor"),
    )
    return jax.shard_map(
        local, mesh=fine, in_specs=placed, out_specs=P("pipe", "tensor"), check_vma=False
    )
```
